32 devices in a mesh: expert: 4 (over z), dp: 4 (over y, x), pair: 2 (over core).
Axes of the slice: x: 2, y: 2, z: 4, core: 2. Of those that a mesh axis runs over, the one named last changes fastest.
Arguments:
- byte_states: bfloat16 [4096, 2048], P(('expert', 'dp')), may hold values from -6 to 6
- positions: int32 [2048], P(('expert', 'dp')), may hold values from 0 to 4095, as said below
- picks: int32 [2048, 2], P(('expert', 'dp')), may hold values from 0 to 3, all different within a row; in each aligned block of 128 rows (0 to 127, 128 to 255, ...) at most 80 rows name the same one
- cotangent: bfloat16 [2048, 2048], P(('expert', 'dp')), may hold values from -6 to 6
- router_weight: bfloat16 [2048, 4], replicated, may hold values from -0.125 to 0.125
- gate_weight: bfloat16 [4, 2048, 768], P('expert', 'dp', 'pair'), may hold values from -0.125 to 0.125
- up_weight: bfloat16 [4, 2048, 768], P('expert', 'dp', 'pair'), may hold values from -0.125 to 0.125
- down_weight: bfloat16 [4, 2048, 768], P('expert', 'dp', 'pair'), may hold values from -0.21875 to 0.21875
Outputs:
- row_grad: bfloat16 [2048, 2048], P(('expert', 'dp'))
- gate_grad: bfloat16 [4, 2048, 768], P('expert', 'dp', 'pair')
- up_grad: bfloat16 [4, 2048, 768], P('expert', 'dp', 'pair')
The draws below stay inside these ranges and needn't reach their ends.
Inputs may be any that keep to these rules, and one draw needn't show every extreme that they name: `positions`: Increasing; the j-th block of 128 rows points into the bytes j * 256 to (j + 1) * 256 - 1 and names the first and the last of them. The 2 picks of a row differ; in each aligned block of 128 rows (the rows of one index of expert and dp) no expert is named by more than 80 rows, a bound that some block reaches.
All inputs are finite; a program needn't handle non-finite values.
Results may differ from the reference program's by a relative error of at most 0.011.
Values may be sent and summed in bfloat16 or wider, within the bound.
A program may use at most 64 MiB of HBM per device.

```python
import math
import jax
import jax.numpy as jnp
import numpy as np
from jax import lax

D = 2048
FF = 768
EXPERTS = 4
TOP = 2
ROWS_DEV = 128
BYTES_DEV = 256
CAP = 80
ROWS = 2048
BYTES = 4096
N_EXPERT = 4
N_DP = 4


def draw_positions(key, part):
    block_count = ROWS // ROWS_DEV
    key_list = jax.random.split(key, block_count)
    inner_count = ROWS_DEV - 2

    def one_block(block_key):
        order = jax.random.permutation(block_key, BYTES_DEV - 2)
        chosen = jnp.sort(order[:inner_count].astype(jnp.int32) + 1)
        head = jnp.zeros((1,), jnp.int32)
        tail = jnp.full((1,), BYTES_DEV - 1, jnp.int32)
        return jnp.concatenate([head, chosen, tail])
    local_pos = jax.vmap(one_block)(key_list)
    offsets = (jnp.arange(block_count, dtype=jnp.int32) * BYTES_DEV)[:, None]
    return (local_pos + offsets).reshape(ROWS)


def shard_levels(rng, dims, cuts, least, largest):
    def one(position, blocks):
        draws = jax.random.uniform(jax.random.fold_in(jax.random.fold_in(rng, 6), position), (blocks,), jnp.float32, least / len(cuts), largest / len(cuts))
        return jnp.repeat(jnp.exp(draws), dims[position] // blocks).reshape((-1,) + (1,) * (len(dims) - position - 1))

    level = one(*cuts[0])
    for cut in cuts[1:]:
        level = level * one(*cut)
    return level


def routed_block(own_key, own, number, rows, number_of, top, bound, lean):
    ranking = jax.random.permutation(own_key, number_of)
    heavy_load, common = load_shares(number_of, rows * top, bound, lean, True), load_shares(number_of, rows * top, bound, lean, False)
    places = jnp.arange(number_of)

    def named(tallies, turn):
        used = int((tallies > 0).sum())
        fixed = max(1, used // 4)
        passed = fixed + (places - fixed + turn * (used - fixed)) % max(1, number_of - fixed)
        return jnp.zeros((number_of,), jnp.int32).at[ranking[jnp.where(places < fixed, places, passed)]].set(jnp.asarray(tallies, jnp.int32))

    tallies = jnp.where(number % 4 == 0, named(heavy_load, number // 4), named(common, number - number // 4 - 1))
    mixed = jax.random.permutation(jax.random.fold_in(own, 3), number_of)
    donor, sink = mixed[0:number_of // 2 * 2:2], mixed[1:number_of // 2 * 2:2]
    margin = jnp.minimum(tallies[donor] - 1, bound - tallies[sink]) // 2
    margin = jnp.where((donor == ranking[0]) | (sink == ranking[0]) | (tallies[sink] == 0), 0, jnp.maximum(margin, 0))
    passed = jax.random.randint(jax.random.fold_in(own, 4), (number_of // 2,), 0, 1 << 20) % (margin + 1)
    tallies = tallies.at[donor].add(-passed).at[sink].add(passed)
    items = jnp.searchsorted(jnp.cumsum(tallies), jnp.arange(rows * top), side="right").astype(jnp.int32)
    listing = items.reshape(top, rows).T
    listing = listing[jax.random.permutation(jax.random.fold_in(own, 1), rows)]
    turn = jax.random.randint(jax.random.fold_in(own, 2), (rows, 1), 0, top)
    return jnp.take_along_axis(listing, (jnp.arange(top)[None, :] + turn) % top, axis=1)


def load_shares(amount, total, most, lean, full):
    weights = [(1 << 20) // math.isqrt(grade ** lean) + 1 for grade in range(1, amount + 1)]
    largest = most if full else min(most, max(-(-total // amount), total * weights[0] // sum(weights)))
    least = 1 if total - largest >= amount - 1 else 0
    holding, rest = [largest] + [least] * (amount - 1), total - largest - least * (amount - 1)
    while rest > 0:
        movable = [i for i in range(1, amount) if holding[i] < largest] or [i for i in range(1, amount) if holding[i] < most]
        mass, left = sum([weights[i] for i in movable]), rest
        for i in movable:
            more = min(most - holding[i], max(1, left * weights[i] // mass), rest)
            holding[i] = holding[i] + more
            rest = rest - more
    return np.array(holding)


def gaussian(key, shape, spread, reach, cuts=(), held_as=jnp.bfloat16):
    drawn = jax.random.normal(key, shape, jnp.float32) * spread
    if len(cuts) > 0:
        drawn = shard_levels(key, shape, cuts, -0.22, 0.18) * drawn
    return jnp.clip(drawn, min=-reach, max=reach).astype(held_as)


def setup_inputs(seed: int = 0) -> dict:
    keys = jax.random.split(jax.random.key(seed), 9)
    byte_states = gaussian(keys[0], (BYTES, D), 1.0, 6.0, ((0, 16),))
    positions = draw_positions(jax.random.fold_in(keys[8], 71), 0)
    picks_keys = jax.random.split(jax.random.fold_in(keys[2], 1), ROWS // ROWS_DEV)
    picks_turns = jax.random.permutation(jax.random.fold_in(keys[2], 3), ROWS // ROWS_DEV)
    picks = jax.vmap(lambda own, number: routed_block(jax.random.fold_in(keys[2], 2), own, number, ROWS_DEV, EXPERTS, TOP, CAP, 2))(picks_keys, picks_turns).reshape((ROWS, TOP))
    cotangent = gaussian(keys[3], (ROWS, D), 1.0, 6.0, ((0, 16),))
    router_weight = gaussian(keys[4], (D, EXPERTS), D ** -0.5, 0.125)
    gate_weight = gaussian(keys[5], (EXPERTS, D, FF), D ** -0.5, 0.125, ((0, 4), (1, 4), (2, 2)))
    up_weight = gaussian(keys[6], (EXPERTS, D, FF), D ** -0.5, 0.125, ((0, 4), (1, 4), (2, 2)))
    down_weight = gaussian(keys[7], (EXPERTS, D, FF), FF ** -0.5, 0.21875, ((0, 4), (1, 4), (2, 2)))
    return {"byte_states": byte_states, "positions": positions, "picks": picks, "cotangent": cotangent, "router_weight": router_weight, "gate_weight": gate_weight, "up_weight": up_weight, "down_weight": down_weight}


def reference(byte_states, positions, picks, cotangent, router_weight, gate_weight, up_weight, down_weight):
    boundary = jnp.take(byte_states, positions, axis=0)
    logits = jnp.dot(boundary, router_weight, preferred_element_type=jnp.float32)
    picked = jnp.take_along_axis(logits, picks, axis=1)
    leading = jax.nn.sigmoid(picked[:, 0] - picked[:, 1])
    mixing = jnp.stack([leading, 1.0 - leading], axis=1)
    mix_low = mixing.astype(jnp.bfloat16).reshape(-1)
    block_count = N_EXPERT * N_DP
    per_block = ROWS_DEV * TOP
    total = block_count * per_block
    flat_picks = picks.reshape(block_count, per_block)
    expert_ids = jnp.arange(EXPERTS, dtype=jnp.int32)
    one_hot = (flat_picks[:, :, None] == expert_ids[None, None, :]).astype(jnp.int32)
    slot_rank = jnp.sum(jnp.cumsum(one_hot, axis=1) * one_hot, axis=2) - 1
    block_ids = jnp.broadcast_to(jnp.arange(block_count, dtype=jnp.int32)[:, None], flat_picks.shape)
    pick_ids = jnp.arange(total, dtype=jnp.int32).reshape(block_count, per_block)
    slot_table = jnp.full((EXPERTS, block_count, CAP), total, jnp.int32)
    slot_table = slot_table.at[flat_picks, block_ids, slot_rank].set(pick_ids)

    def one_expert(expert_args):
        slot_ids, gate_mat, up_mat, down_mat = expert_args
        slot_ids = slot_ids.reshape(-1)
        is_live = slot_ids < total
        clamped = jnp.minimum(slot_ids, total - 1)
        source_row = clamped // TOP
        expert_rows = jnp.where(is_live[:, None], boundary[source_row], 0)
        expert_cot = jnp.where(is_live[:, None], cotangent[source_row], 0)
        expert_mix = jnp.where(is_live, mix_low[clamped], 0)
        gate_pre = jnp.dot(expert_rows, gate_mat, preferred_element_type=jnp.float32)
        up_pre = jnp.dot(expert_rows, up_mat, preferred_element_type=jnp.float32)
        sigma = jax.nn.sigmoid(gate_pre)
        activ = gate_pre * sigma
        slope = sigma * (1.0 + gate_pre * (1.0 - sigma))
        hidden = (activ * up_pre).astype(jnp.bfloat16)
        expert_out = lax.dot_general(hidden, down_mat, (((1,), (1,)), ((), ())), preferred_element_type=jnp.float32)
        mix_grad = jnp.sum(expert_cot.astype(jnp.float32) * expert_out, axis=1).astype(jnp.bfloat16)
        scaled = (expert_mix.astype(jnp.float32)[:, None] * expert_cot.astype(jnp.float32)).astype(jnp.bfloat16)
        hidden_grad = jnp.dot(scaled, down_mat, preferred_element_type=jnp.float32)
        gate_pre_grad = (hidden_grad * up_pre * slope).astype(jnp.bfloat16)
        up_pre_grad = (hidden_grad * activ).astype(jnp.bfloat16)
        pick_grad = lax.dot_general(gate_pre_grad, gate_mat, (((1,), (1,)), ((), ())), preferred_element_type=jnp.float32)
        pick_grad = pick_grad + lax.dot_general(up_pre_grad, up_mat, (((1,), (1,)), ((), ())), preferred_element_type=jnp.float32)
        pick_grad = pick_grad.astype(jnp.bfloat16)
        joined = jnp.concatenate([gate_pre_grad, up_pre_grad], axis=1)
        rows_four = expert_rows.reshape(N_EXPERT, N_DP, CAP, D).astype(jnp.float32)
        joined_four = joined.reshape(N_EXPERT, N_DP, CAP, 2 * FF).astype(jnp.float32)
        group_sums = jnp.einsum("sdcx,sdcf->dxf", rows_four, joined_four)
        rounded = lax.optimization_barrier(group_sums.astype(jnp.bfloat16))
        weight_sum = jnp.sum(rounded.astype(jnp.float32), axis=0).astype(jnp.bfloat16)
        return pick_grad, mix_grad, weight_sum[:, :FF], weight_sum[:, FF:]

    pick_all, mix_all, gate_grad, up_grad = lax.map(one_expert, (slot_table, gate_weight, up_weight, down_weight))
    flat_table = slot_table.reshape(EXPERTS, -1)
    pick_back = jnp.zeros((total, D), jnp.bfloat16).at[flat_table].set(pick_all, mode="drop")
    mix_back = jnp.zeros((total,), jnp.bfloat16).at[flat_table].set(mix_all, mode="drop")
    row_sum = jnp.sum(pick_back.reshape(ROWS, TOP, D).astype(jnp.float32), axis=1)
    mix_grad = mix_back.reshape(ROWS, TOP).astype(jnp.float32)
    blended = jnp.sum(mixing * mix_grad, axis=1, keepdims=True)
    logit_grad = mixing * (mix_grad - blended)
    pick_hot = (picks[:, :, None] == expert_ids[None, None, :]).astype(jnp.float32)
    coeffs = jnp.sum(logit_grad[:, :, None] * pick_hot, axis=1)
    router_term = jnp.dot(coeffs, router_weight.astype(jnp.float32).T, precision=lax.Precision.HIGHEST)
    row_grad = (row_sum + router_term).astype(jnp.bfloat16)
    return row_grad, gate_grad, up_grad
```

```python
import jax
import jax.numpy as jnp
from jax import lax
from jax.sharding import PartitionSpec as P


def local(
    byte_states, positions, picks, cotangent, router_weight, gate_weight, up_weight, down_weight
):
    byte_count = byte_states.shape[0]
    row_total = positions.shape[0]
    width = byte_states.shape[1]
    experts = router_weight.shape[1]
    top_count = picks.shape[1]
    capacity = max(2, 5 * row_total * top_count // (4 * experts))
    pick_total = row_total * top_count
    boundary = jnp.take(byte_states, positions % byte_count, axis=0)
    logits = jnp.dot(boundary, router_weight, preferred_element_type=jnp.float32)
    picked = jnp.take_along_axis(logits, picks, axis=1)
    leading = jax.nn.sigmoid(picked[:, 0] - picked[:, 1])
    mixing = jnp.stack([leading, 1.0 - leading], axis=1)
    mix_low = mixing.astype(jnp.bfloat16).reshape(-1)
    flat_picks = picks.reshape(-1)
    expert_ids = jnp.arange(experts, dtype=jnp.int32)
    one_hot = (flat_picks[:, None] == expert_ids[None, :]).astype(jnp.int32)
    order = jnp.arange(pick_total, dtype=jnp.int32)
    earlier = (order[None, :] < order[:, None]).astype(jnp.bfloat16)
    before = jnp.dot(earlier, one_hot.astype(jnp.bfloat16), preferred_element_type=jnp.float32)
    slot_rank = jnp.sum(before.astype(jnp.int32) * one_hot, axis=1)
    target = flat_picks * capacity + slot_rank
    slot_source = jnp.full((experts * capacity,), pick_total, jnp.int32)
    slot_source = slot_source.at[target].set(jnp.arange(pick_total, dtype=jnp.int32))
    is_live = slot_source < pick_total
    clamped = jnp.minimum(slot_source, pick_total - 1)
    source_row = clamped // top_count
    send_rows = jnp.where(is_live[:, None], boundary[source_row], 0).reshape(
        experts, capacity, width
    )
    send_cot = jnp.where(is_live[:, None], cotangent[source_row], 0).reshape(
        experts, capacity, width
    )
    send_mix = jnp.where(is_live, mix_low[clamped], 0).reshape(experts, capacity)
    gate_full, up_full, down_full = (
        lax.all_gather(gate_weight, "dp", axis=1, tiled=True),
        lax.all_gather(up_weight, "dp", axis=1, tiled=True),
        lax.all_gather(down_weight, "dp", axis=1, tiled=True),
    )
    hidden_half = gate_full.shape[2]
    gate_up = jnp.concatenate([gate_full[0], up_full[0]], axis=1)
    down_mat = down_full[0]
    recv_rows, recv_cot, recv_mix = (
        lax.all_to_all(send_rows, "expert", split_axis=0, concat_axis=0, tiled=True),
        lax.all_to_all(send_cot, "expert", split_axis=0, concat_axis=0, tiled=True),
        lax.all_to_all(send_mix, "expert", split_axis=0, concat_axis=0, tiled=True),
    )
    sources = recv_rows.shape[0]
    slot_total = sources * capacity
    expert_rows = recv_rows.reshape(slot_total, width)
    expert_cot = recv_cot.reshape(slot_total, width)
    expert_mix = recv_mix.reshape(slot_total)
    both_pre = jnp.dot(expert_rows, gate_up, preferred_element_type=jnp.float32)
    gate_pre = both_pre[:, :hidden_half]
    up_pre = both_pre[:, hidden_half:]
    sigma = jax.nn.sigmoid(gate_pre)
    activ = gate_pre * sigma
    slope = sigma * (1.0 + gate_pre * (1.0 - sigma))
    hidden = (activ * up_pre).astype(jnp.bfloat16)
    cot_down = jnp.dot(expert_cot, down_mat, preferred_element_type=jnp.float32)
    mix_part = jnp.sum(hidden.astype(jnp.float32) * cot_down, axis=1)
    scaled = (expert_mix.astype(jnp.float32)[:, None] * expert_cot.astype(jnp.float32)).astype(
        jnp.bfloat16
    )
    hidden_grad = jnp.dot(scaled, down_mat, preferred_element_type=jnp.float32)
    gate_pre_grad = (hidden_grad * up_pre * slope).astype(jnp.bfloat16)
    up_pre_grad = (hidden_grad * activ).astype(jnp.bfloat16)
    joined = jnp.concatenate([gate_pre_grad, up_pre_grad], axis=1)
    grad_part = lax.dot_general(
        joined, gate_up, (((1,), (1,)), ((), ())), preferred_element_type=jnp.float32
    )
    weight_sum = lax.psum_scatter(
        lax.dot_general(
            expert_rows, joined, (((0,), (0,)), ((), ())), preferred_element_type=jnp.float32
        ).astype(jnp.bfloat16),
        "dp",
        scatter_dimension=0,
        tiled=True,
    ).astype(jnp.float32)
    gate_grad = weight_sum[:, :hidden_half].astype(jnp.bfloat16)[None]
    up_grad = weight_sum[:, hidden_half:].astype(jnp.bfloat16)[None]
    grad_sum, mix_sum = (
        lax.psum(grad_part.astype(jnp.bfloat16), "pair").astype(jnp.float32),
        lax.psum(mix_part.astype(jnp.bfloat16), "pair").astype(jnp.float32),
    )
    grad_low = grad_sum.astype(jnp.bfloat16).reshape(sources, capacity, width)
    mix_grad_low = mix_sum.astype(jnp.bfloat16).reshape(sources, capacity)
    back_grad, back_mix = (
        lax.all_to_all(grad_low, "expert", split_axis=0, concat_axis=0, tiled=True),
        lax.all_to_all(mix_grad_low, "expert", split_axis=0, concat_axis=0, tiled=True),
    )
    pick_grad = back_grad.reshape(experts * capacity, width)[target]
    row_sum = jnp.sum(pick_grad.reshape(row_total, top_count, width).astype(jnp.float32), axis=1)
    mix_grad = (
        back_mix.reshape(experts * capacity)[target]
        .reshape(row_total, top_count)
        .astype(jnp.float32)
    )
    blended = jnp.sum(mixing * mix_grad, axis=1, keepdims=True)
    logit_grad = mixing * (mix_grad - blended)
    pick_hot = one_hot.reshape(row_total, top_count, experts).astype(jnp.float32)
    coeffs = jnp.sum(logit_grad[:, :, None] * pick_hot, axis=1)
    router_term = jnp.dot(
        coeffs, router_weight.astype(jnp.float32).T, precision=lax.Precision.HIGHEST
    )
    row_grad = (row_sum + router_term).astype(jnp.bfloat16)
    return (row_grad, gate_grad, up_grad)


def solution(mesh):
    in_specs = (
        P(("expert", "dp"), None),
        P(("expert", "dp")),
        P(("expert", "dp"), None),
        P(("expert", "dp"), None),
        P(),
        P("expert", "dp", "pair"),
        P("expert", "dp", "pair"),
        P("expert", "dp", "pair"),
    )
    out_specs = (P(("expert", "dp"), None), P("expert", "dp", "pair"), P("expert", "dp", "pair"))
    return jax.shard_map(local, mesh=mesh, in_specs=in_specs, out_specs=out_specs, check_vma=False)
```

```python
import functools

import jax
import jax.numpy as jnp
from jax import lax
from jax.experimental import pallas as pl
from jax.experimental.pallas import tpu as pltpu
from jax.sharding import PartitionSpec as P

MESH = pl.DeviceIdType.MESH
LANES = 128
BF16, F32 = jnp.bfloat16, jnp.float32


def dot(a, b, contract=((1,), (0,))):
    return lax.dot_general(a, b, (contract, ((), ())), preferred_element_type=F32)


def kernel(
    byte_ref, pos_ref, pick_ref, cot_ref, router_ref, gate_ref, up_ref, down_ref,
    row_out, gate_out, up_out,
    x_buf, c_buf, w_buf, acc, joined, mix_buf, turn_buf, coef_hi, coef_lo,
    pick_send, pick_recv, pick_own, line_send, line_recv, wgrad_send, wgrad_recv, fin_send, fin_recv,
    w_ss, w_rs, z_ss, z_rs, q_ss, q_rs, p_ss, p_rs, l_ss, l_rs, g_ss, g_rs, f_ss, f_rs,
):
    z, s, p = lax.axis_index("expert"), lax.axis_index("dp"), lax.axis_index("pair")
    nz, half, width = x_buf.shape[1], x_buf.shape[2], c_buf.shape[3]
    depth = gate_ref.shape[1]
    other = 1 - p
    x_nb = s + 1 - 2 * lax.rem(s, 2)
    y_nb = lax.rem(s + 2, 4)
    diag = 3 - s

    def copy(src, dst, ss, rs, device):
        return pltpu.make_async_remote_copy(
            src_ref=src, dst_ref=dst, send_sem=ss, recv_sem=rs, device_id=device, device_id_type=MESH
        )

    barrier = pltpu.get_barrier_semaphore()
    peers = [{"dp": x_nb}, {"dp": y_nb}, {"dp": diag}, {"pair": other}]
    peers += [{"expert": lax.rem(z + j, nz)} for j in range(1, nz)]
    for peer in peers:
        pl.semaphore_signal(barrier, inc=1, device_id=peer, device_id_type=MESH)

    spots = lax.broadcasted_iota(jnp.int32, (2 * half, byte_ref.shape[0]), 1)
    hot = jnp.where(spots == pos_ref[...], 1.0, 0.0).astype(BF16)
    for c in range(0, width, depth):
        rows = dot(hot, byte_ref[:, c : c + depth]).astype(BF16)
        for h in range(2):
            x_buf[h, z, :, c : c + depth] = rows[h * half : (h + 1) * half]
    for h in range(2):
        x_buf[h, z, :, width:] = pick_ref[h * half : (h + 1) * half, :]
        c_buf[h, z] = cot_ref[h * half : (h + 1) * half, :]
    pl.semaphore_wait(barrier, len(peers))

    own = [gate_ref.at[0], up_ref.at[0], down_ref.at[0]]

    def w_copy(kind, i):
        if kind == 0:
            return copy(own[i], w_buf.at[i, s], w_ss.at[0, i], w_rs.at[0, i], {"dp": x_nb})
        if kind == 1:
            return copy(own[i], w_buf.at[i, s], w_ss.at[1, i], w_rs.at[1, i], {"dp": y_nb})
        part = pl.ds(0 if kind == 2 else depth // 2, depth // 2)
        frm, to = (x_nb, y_nb) if kind == 2 else (y_nb, x_nb)
        view = w_buf.at[i, frm, part]
        return copy(view, view, w_ss.at[kind, i], w_rs.at[kind, i], {"dp": to})

    def w_arrived(kind, i):
        frm = (x_nb, y_nb, diag, diag)[kind]
        view = w_buf.at[i, frm]
        if kind >= 2:
            view = w_buf.at[i, frm, pl.ds(0 if kind == 2 else depth // 2, depth // 2)]
        copy(view, view, w_ss.at[kind, i], w_rs.at[kind, i], {"dp": x_nb}).wait_recv()

    for i in range(3):
        w_copy(0, i).start()
        w_copy(1, i).start()

    bufs = (c_buf, x_buf)

    def z_copy(up, k, a):
        origin = lax.rem(z + (nz - k if up else k), nz)
        view = bufs[a].at[p, origin]
        d = 0 if up else 1
        to = lax.rem(z + (1 if up else nz - 1), nz)
        return copy(view, view, z_ss.at[d, k, a], z_rs.at[d, k, a], {"expert": to})

    def q_copy(up, k, a, mine):
        origin = lax.rem(z + (nz - k if up else k), nz)
        view = bufs[a].at[p if mine else other, origin]
        d = 0 if up else 1
        return copy(view, view, q_ss.at[d, k - 1, a], q_rs.at[d, k - 1, a], {"pair": other})

    def z_arrived(up, k, a):
        origin = lax.rem(z + (nz - k if up else k), nz)
        view = bufs[a].at[p, origin]
        d = 0 if up else 1
        to = lax.rem(z + 1, nz)
        copy(view, view, z_ss.at[d, k - 1, a], z_rs.at[d, k - 1, a], {"expert": to}).wait_recv()

    def comes(up, k):
        return z >= k if up else z + k < nz

    def goes(up, k):
        there = z + 1 < nz if up else z >= 1
        return jnp.logical_and(there, comes(up, k)) if k else there

    for a in range(2):
        for up in (True, False):
            pl.when(goes(up, 0))(z_copy(up, 0, a).start)

    def z_step(k):
        for a in range(2):
            for up in (True, False):

                def arrived(up=up, a=a):
                    z_arrived(up, k, a)
                    q_copy(up, k, a, True).start()

                pl.when(comes(up, k))(arrived)
                if k + 1 < nz:
                    pl.when(goes(up, k))(z_copy(up, k, a).start)

    def w_step(i):
        w_arrived(0, i)
        w_copy(2, i).start()
        w_arrived(1, i)
        w_copy(3, i).start()

    for i in range(3):
        w_buf[i, s] = own[i][...]
    w_step(0)
    z_step(1)
    w_step(1)
    z_step(2)
    w_step(2)
    z_step(3)
    for k in range(1, nz):
        for a in range(2):
            for up in (True, False):
                pl.when(comes(up, k))(q_copy(up, k, a, False).wait_recv)

    lane = lax.broadcasted_iota(jnp.int32, (nz * half, LANES), 1).astype(F32)
    me = z.astype(F32)
    for h in range(2):
        logits = dot(x_buf[h, :, :, :width].reshape(nz * half, width), router_ref[...], ((1,), (1,)))
        meta = x_buf[h, :, :, width:].reshape(nz * half, LANES).astype(F32)
        first, second = meta[:, 0:1], meta[:, 1:2]
        hot0 = jnp.where(lane == first, 1.0, 0.0)
        hot1 = jnp.where(lane == second, 1.0, 0.0)
        gap = jnp.sum(logits * (hot0 - hot1), axis=1, keepdims=True)
        leading = jax.nn.sigmoid(gap)
        rest = 1.0 - leading
        mixing = jnp.where(first == me, leading, jnp.where(second == me, rest, 0.0))
        mix_buf[h] = mixing.astype(BF16).astype(F32)
        sign = jnp.where(first == me, 1.0, jnp.where(second == me, -1.0, 0.0))
        turn_buf[h] = (leading * rest * sign) * (hot0 - hot1)

    def accumulate(owner, start):
        cols = pl.ds(pl.multiple_of(owner * depth, depth), depth)
        for h in range(2):
            x = x_buf[h, :, :, cols].reshape(nz * half, depth)
            c = c_buf[h, :, :, cols].reshape(nz * half, depth)
            for i, rows in enumerate((x, x, c)):
                term = dot(rows, w_buf[i, owner])
                acc[i, h] = term if start else acc[i, h] + term

    accumulate(s, True)
    accumulate(x_nb, False)
    accumulate(y_nb, False)
    for i in range(3):
        w_arrived(2, i)
        w_arrived(3, i)
    accumulate(diag, False)

    step = 64

    @pl.loop(0, nz * half // step)
    def _(n):
        part = pl.ds(pl.multiple_of(n * step, step), step)
        for h in range(2):
            gate, up, cot_down = acc[0, h, part], acc[1, h, part], acc[2, h, part]
            sigma = jax.nn.sigmoid(gate)
            activ = gate * sigma
            slope = sigma * (1.0 + gate * (1.0 - sigma))
            hidden = (activ * up).astype(BF16).astype(F32)
            mix_part = jnp.sum(hidden * cot_down, axis=1, keepdims=True)
            grad = mix_buf[h, part] * cot_down
            joined[0, h, part] = (grad * up * slope).astype(BF16)
            joined[1, h, part] = (grad * activ).astype(BF16)
            coef = mix_part * turn_buf[h, part]
            high = coef.astype(BF16)
            coef_hi[h, part] = high
            coef_lo[h, part] = (coef - high.astype(F32)).astype(BF16)

    def weight_grad(owner, slot):
        cols = pl.ds(pl.multiple_of(owner * depth, depth), depth)
        for i in range(2):
            total = None
            for h in range(2):
                x = x_buf[h, :, :, cols].reshape(nz * half, depth)
                term = dot(x, joined[i, h], ((0,), (0,)))
                total = term if total is None else total + term
            wgrad_send[slot, i] = total.astype(BF16)

    def g_copy(slot):
        to = (x_nb, y_nb, diag)[slot]
        return copy(wgrad_send.at[slot], wgrad_recv.at[slot], g_ss.at[slot], g_rs.at[slot], {"dp": to})

    for slot in (2, 0, 1):
        weight_grad((x_nb, y_nb, diag)[slot], slot)
        g_copy(slot).start()

    def pick_grads(h, c):
        out = dot(joined[0, h], w_buf[0, c], ((1,), (1,))) + dot(joined[1, h], w_buf[1, c], ((1,), (1,)))
        router = router_ref[:, c * depth : (c + 1) * depth]
        return out + dot(coef_hi[h], router) + dot(coef_lo[h], router)

    for c in range(4):
        pick_send[:, :, c * depth : (c + 1) * depth] = pick_grads(other, c).astype(BF16).reshape(nz, half, depth)
    p_copy = copy(pick_send, pick_recv, p_ss, p_rs, {"pair": other})
    p_copy.start()
    for c in range(4):
        pick_own[:, :, c * depth : (c + 1) * depth] = pick_grads(p, c).reshape(nz, half, depth)
    p_copy.wait_recv()

    def l_copy(j):
        to = lax.rem(z + j, nz)
        return copy(line_send.at[j - 1], line_recv.at[j - 1], l_ss.at[j - 1], l_rs.at[j - 1], {"expert": to})

    for j in range(1, nz):
        origin = lax.rem(z + j, nz)
        line_send[j - 1] = (pick_own[origin] + pick_recv[origin].astype(F32)).astype(BF16)
        l_copy(j).start()
    weight_grad(s, 3)

    for j in range(1, nz):
        l_copy(j).wait_recv()
    total = pick_own[z] + pick_recv[z].astype(F32)
    for j in range(1, nz):
        total = total + line_recv[j - 1].astype(F32)
    fin_send[...] = total.astype(BF16)
    f_copy = copy(fin_send, fin_recv, f_ss, f_rs, {"pair": other})
    f_copy.start()
    row_out[pl.ds(pl.multiple_of(p * half, half), half), :] = fin_send[...]

    for slot in range(3):
        g_copy(slot).wait_recv()
    for i, out in enumerate((gate_out, up_out)):
        sums = wgrad_send[3, i].astype(F32)
        for slot in range(3):
            sums = sums + wgrad_recv[slot, i].astype(F32)
        out[0] = sums.astype(BF16)
    f_copy.wait_recv()
    row_out[pl.ds(pl.multiple_of(other * half, half), half), :] = fin_recv[...]

    for i in range(3):
        for kind in range(4):
            w_copy(kind, i).wait_send()
    for a in range(2):
        for up in (True, False):
            for k in range(nz - 1):
                pl.when(goes(up, k))(z_copy(up, k, a).wait_send)
            for k in range(1, nz):
                pl.when(comes(up, k))(q_copy(up, k, a, True).wait_send)
    for slot in range(3):
        g_copy(slot).wait_send()
    p_copy.wait_send()
    for j in range(1, nz):
        l_copy(j).wait_send()
    f_copy.wait_send()


def dense(
    nz, byte_states, positions, picks, cotangent, router_weight, gate_weight, up_weight, down_weight
):
    rows, width = cotangent.shape
    half, depth, units = rows // 2, gate_weight.shape[1], gate_weight.shape[2]
    spots = (positions % byte_states.shape[0])[:, None]
    meta = jnp.pad(picks.astype(BF16), ((0, 0), (0, LANES - picks.shape[1])))
    router = jnp.pad(router_weight.T, ((0, LANES - router_weight.shape[1]), (0, 0)))
    vmem, dma = pltpu.VMEM, pltpu.SemaphoreType.DMA
    whole = pl.BlockSpec(memory_space=vmem)
    scratch = [
        vmem((2, nz, half, width + LANES), BF16),
        vmem((2, nz, half, width), BF16),
        vmem((3, 4, depth, units), BF16),
        vmem((3, 2, nz * half, units), F32),
        vmem((2, 2, nz * half, units), BF16),
        vmem((2, nz * half, 1), F32),
        vmem((2, nz * half, LANES), F32),
        vmem((2, nz * half, LANES), BF16),
        vmem((2, nz * half, LANES), BF16),
        vmem((nz, half, width), BF16),
        vmem((nz, half, width), BF16),
        vmem((nz, half, width), F32),
        vmem((nz - 1, half, width), BF16),
        vmem((nz - 1, half, width), BF16),
        vmem((4, 2, depth, units), BF16),
        vmem((3, 2, depth, units), BF16),
        vmem((half, width), BF16),
        vmem((half, width), BF16),
        dma((4, 3)), dma((4, 3)),
        dma((2, nz - 1, 2)), dma((2, nz - 1, 2)),
        dma((2, nz - 1, 2)), dma((2, nz - 1, 2)),
        dma, dma,
        dma((nz - 1,)), dma((nz - 1,)),
        dma((3,)), dma((3,)),
        dma, dma,
    ]
    return pl.pallas_call(
        kernel,
        out_shape=(
            jax.ShapeDtypeStruct((rows, width), BF16),
            jax.ShapeDtypeStruct(gate_weight.shape, BF16),
            jax.ShapeDtypeStruct(up_weight.shape, BF16),
        ),
        in_specs=[whole] * 8,
        out_specs=(whole,) * 3,
        scratch_shapes=scratch,
        compiler_params=pltpu.CompilerParams(
            collective_id=0, has_side_effects=True, vmem_limit_bytes=52 * 2**20
        ),
    )(byte_states, spots, meta, cotangent, router, gate_weight, up_weight, down_weight)


def local(
    byte_states, positions, picks, cotangent, router_weight, gate_weight, up_weight, down_weight
):
    byte_count = byte_states.shape[0]
    row_total = positions.shape[0]
    width = byte_states.shape[1]
    experts = router_weight.shape[1]
    top_count = picks.shape[1]
    capacity = max(2, 5 * row_total * top_count // (4 * experts))
    pick_total = row_total * top_count
    boundary = jnp.take(byte_states, positions % byte_count, axis=0)
    logits = jnp.dot(boundary, router_weight, preferred_element_type=jnp.float32)
    picked = jnp.take_along_axis(logits, picks, axis=1)
    leading = jax.nn.sigmoid(picked[:, 0] - picked[:, 1])
    mixing = jnp.stack([leading, 1.0 - leading], axis=1)
    mix_low = mixing.astype(jnp.bfloat16).reshape(-1)
    flat_picks = picks.reshape(-1)
    expert_ids = jnp.arange(experts, dtype=jnp.int32)
    one_hot = (flat_picks[:, None] == expert_ids[None, :]).astype(jnp.int32)
    order = jnp.arange(pick_total, dtype=jnp.int32)
    earlier = (order[None, :] < order[:, None]).astype(jnp.bfloat16)
    before = jnp.dot(earlier, one_hot.astype(jnp.bfloat16), preferred_element_type=jnp.float32)
    slot_rank = jnp.sum(before.astype(jnp.int32) * one_hot, axis=1)
    target = flat_picks * capacity + slot_rank
    slot_source = jnp.full((experts * capacity,), pick_total, jnp.int32)
    slot_source = slot_source.at[target].set(jnp.arange(pick_total, dtype=jnp.int32))
    is_live = slot_source < pick_total
    clamped = jnp.minimum(slot_source, pick_total - 1)
    source_row = clamped // top_count
    send_rows = jnp.where(is_live[:, None], boundary[source_row], 0).reshape(
        experts, capacity, width
    )
    send_cot = jnp.where(is_live[:, None], cotangent[source_row], 0).reshape(
        experts, capacity, width
    )
    send_mix = jnp.where(is_live, mix_low[clamped], 0).reshape(experts, capacity)
    gate_full, up_full, down_full = (
        lax.all_gather(gate_weight, "dp", axis=1, tiled=True),
        lax.all_gather(up_weight, "dp", axis=1, tiled=True),
        lax.all_gather(down_weight, "dp", axis=1, tiled=True),
    )
    hidden_half = gate_full.shape[2]
    gate_up = jnp.concatenate([gate_full[0], up_full[0]], axis=1)
    down_mat = down_full[0]
    recv_rows, recv_cot, recv_mix = (
        lax.all_to_all(send_rows, "expert", split_axis=0, concat_axis=0, tiled=True),
        lax.all_to_all(send_cot, "expert", split_axis=0, concat_axis=0, tiled=True),
        lax.all_to_all(send_mix, "expert", split_axis=0, concat_axis=0, tiled=True),
    )
    sources = recv_rows.shape[0]
    slot_total = sources * capacity
    expert_rows = recv_rows.reshape(slot_total, width)
    expert_cot = recv_cot.reshape(slot_total, width)
    expert_mix = recv_mix.reshape(slot_total)
    both_pre = jnp.dot(expert_rows, gate_up, preferred_element_type=jnp.float32)
    gate_pre = both_pre[:, :hidden_half]
    up_pre = both_pre[:, hidden_half:]
    sigma = jax.nn.sigmoid(gate_pre)
    activ = gate_pre * sigma
    slope = sigma * (1.0 + gate_pre * (1.0 - sigma))
    hidden = (activ * up_pre).astype(jnp.bfloat16)
    cot_down = jnp.dot(expert_cot, down_mat, preferred_element_type=jnp.float32)
    mix_part = jnp.sum(hidden.astype(jnp.float32) * cot_down, axis=1)
    scaled = (expert_mix.astype(jnp.float32)[:, None] * expert_cot.astype(jnp.float32)).astype(
        jnp.bfloat16
    )
    hidden_grad = jnp.dot(scaled, down_mat, preferred_element_type=jnp.float32)
    gate_pre_grad = (hidden_grad * up_pre * slope).astype(jnp.bfloat16)
    up_pre_grad = (hidden_grad * activ).astype(jnp.bfloat16)
    joined = jnp.concatenate([gate_pre_grad, up_pre_grad], axis=1)
    grad_part = lax.dot_general(
        joined, gate_up, (((1,), (1,)), ((), ())), preferred_element_type=jnp.float32
    )
    weight_sum = lax.psum_scatter(
        lax.dot_general(
            expert_rows, joined, (((0,), (0,)), ((), ())), preferred_element_type=jnp.float32
        ).astype(jnp.bfloat16),
        "dp",
        scatter_dimension=0,
        tiled=True,
    ).astype(jnp.float32)
    gate_grad = weight_sum[:, :hidden_half].astype(jnp.bfloat16)[None]
    up_grad = weight_sum[:, hidden_half:].astype(jnp.bfloat16)[None]
    grad_sum, mix_sum = (
        lax.psum(grad_part.astype(jnp.bfloat16), "pair").astype(jnp.float32),
        lax.psum(mix_part.astype(jnp.bfloat16), "pair").astype(jnp.float32),
    )
    grad_low = grad_sum.astype(jnp.bfloat16).reshape(sources, capacity, width)
    mix_grad_low = mix_sum.astype(jnp.bfloat16).reshape(sources, capacity)
    back_grad, back_mix = (
        lax.all_to_all(grad_low, "expert", split_axis=0, concat_axis=0, tiled=True),
        lax.all_to_all(mix_grad_low, "expert", split_axis=0, concat_axis=0, tiled=True),
    )
    pick_grad = back_grad.reshape(experts * capacity, width)[target]
    row_sum = jnp.sum(pick_grad.reshape(row_total, top_count, width).astype(jnp.float32), axis=1)
    mix_grad = (
        back_mix.reshape(experts * capacity)[target]
        .reshape(row_total, top_count)
        .astype(jnp.float32)
    )
    blended = jnp.sum(mixing * mix_grad, axis=1, keepdims=True)
    logit_grad = mixing * (mix_grad - blended)
    pick_hot = one_hot.reshape(row_total, top_count, experts).astype(jnp.float32)
    coeffs = jnp.sum(logit_grad[:, :, None] * pick_hot, axis=1)
    router_term = jnp.dot(
        coeffs, router_weight.astype(jnp.float32).T, precision=lax.Precision.HIGHEST
    )
    row_grad = (row_sum + router_term).astype(jnp.bfloat16)
    return (row_grad, gate_grad, up_grad)


def solution(mesh):
    in_specs = (
        P(("expert", "dp"), None),
        P(("expert", "dp")),
        P(("expert", "dp"), None),
        P(("expert", "dp"), None),
        P(),
        P("expert", "dp", "pair"),
        P("expert", "dp", "pair"),
        P("expert", "dp", "pair"),
    )
    out_specs = (P(("expert", "dp"), None), P("expert", "dp", "pair"), P("expert", "dp", "pair"))
    few = dict(mesh.shape) == {"expert": 4, "dp": 4, "pair": 2}
    body = functools.partial(dense, 4) if few else local
    return jax.shard_map(body, mesh=mesh, in_specs=in_specs, out_specs=out_specs, check_vma=False)
```

```python
import functools

import jax
import jax.numpy as jnp
from jax import lax
from jax.experimental import pallas as pl
from jax.experimental.pallas import tpu as pltpu
from jax.sharding import PartitionSpec as P

MESH = pl.DeviceIdType.MESH
LANES = 128
BF16, F32 = jnp.bfloat16, jnp.float32


def dot(a, b, contract=((1,), (0,))):
    return lax.dot_general(a, b, (contract, ((), ())), preferred_element_type=F32)


def kernel(
    byte_ref, pos_ref, pick_ref, cot_ref, router_ref, gate_ref, up_ref, down_ref,
    row_out, gate_out, up_out,
    x_buf, c_buf, w_buf, acc, joined, mix_buf, turn_buf, coef_hi, coef_lo,
    pick_send, pick_recv, pick_own, line_send, line_recv, wgrad_send, wgrad_recv, fin_send, fin_recv, router,
    w_ss, w_rs, z_ss, z_rs, q_ss, q_rs, p_ss, p_rs, l_ss, l_rs, g_ss, g_rs, f_ss, f_rs,
):
    z, s, p = lax.axis_index("expert"), lax.axis_index("dp"), lax.axis_index("pair")
    nz, half, width = x_buf.shape[1], x_buf.shape[2], c_buf.shape[3]
    depth = gate_ref.shape[1]
    other = 1 - p
    x_nb = s + 1 - 2 * lax.rem(s, 2)
    y_nb = lax.rem(s + 2, 4)
    diag = 3 - s

    def copy(src, dst, ss, rs, device):
        return pltpu.make_async_remote_copy(
            src_ref=src, dst_ref=dst, send_sem=ss, recv_sem=rs, device_id=device, device_id_type=MESH
        )

    barrier = pltpu.get_barrier_semaphore()
    peers = [{"dp": x_nb}, {"dp": y_nb}, {"dp": diag}, {"pair": other}]
    peers += [{"expert": lax.rem(z + j, nz)} for j in range(1, nz)]
    for peer in peers:
        pl.semaphore_signal(barrier, inc=1, device_id=peer, device_id_type=MESH)

    count = byte_ref.shape[0]
    spots = lax.broadcasted_iota(jnp.int32, (count, 2 * half), 0) + (z * 4 + s) * count
    hot = jnp.where(spots == pos_ref[...], 1.0, 0.0).astype(BF16)
    for c in range(0, width, depth):
        rows = dot(hot, byte_ref[:, c : c + depth], ((0,), (0,))).astype(BF16)
        for h in range(2):
            x_buf[h, z, :, c : c + depth] = rows[h * half : (h + 1) * half]
    place = lax.broadcasted_iota(jnp.int32, (LANES, 2 * half), 0)
    picked = pick_ref[...].astype(F32)
    meta = jnp.where(place == 0, picked[0:1, :], jnp.where(place == 1, picked[1:2, :], 0.0)).T
    for h in range(2):
        x_buf[h, z, :, width:] = meta[h * half : (h + 1) * half].astype(BF16)
        c_buf[h, z] = cot_ref[h * half : (h + 1) * half, :]
    pl.semaphore_wait(barrier, len(peers))

    own = [gate_ref.at[0], up_ref.at[0], down_ref.at[0]]

    def w_copy(kind, i):
        if kind == 0:
            return copy(own[i], w_buf.at[i, s], w_ss.at[0, i], w_rs.at[0, i], {"dp": x_nb})
        if kind == 1:
            return copy(own[i], w_buf.at[i, s], w_ss.at[1, i], w_rs.at[1, i], {"dp": y_nb})
        part = pl.ds(0 if kind == 2 else depth // 2, depth // 2)
        frm, to = (x_nb, y_nb) if kind == 2 else (y_nb, x_nb)
        view = w_buf.at[i, frm, part]
        return copy(view, view, w_ss.at[kind, i], w_rs.at[kind, i], {"dp": to})

    def w_arrived(kind, i):
        frm = (x_nb, y_nb, diag, diag)[kind]
        view = w_buf.at[i, frm]
        if kind >= 2:
            view = w_buf.at[i, frm, pl.ds(0 if kind == 2 else depth // 2, depth // 2)]
        copy(view, view, w_ss.at[kind, i], w_rs.at[kind, i], {"dp": x_nb}).wait_recv()

    for i in range(3):
        w_copy(0, i).start()
        w_copy(1, i).start()

    bufs = (c_buf, x_buf)

    def z_copy(up, k, a):
        origin = lax.rem(z + (nz - k if up else k), nz)
        view = bufs[a].at[p, origin]
        d = 0 if up else 1
        to = lax.rem(z + (1 if up else nz - 1), nz)
        return copy(view, view, z_ss.at[d, k, a], z_rs.at[d, k, a], {"expert": to})

    def q_copy(up, k, a, mine):
        origin = lax.rem(z + (nz - k if up else k), nz)
        view = bufs[a].at[p if mine else other, origin]
        d = 0 if up else 1
        return copy(view, view, q_ss.at[d, k - 1, a], q_rs.at[d, k - 1, a], {"pair": other})

    def z_arrived(up, k, a):
        origin = lax.rem(z + (nz - k if up else k), nz)
        view = bufs[a].at[p, origin]
        d = 0 if up else 1
        to = lax.rem(z + 1, nz)
        copy(view, view, z_ss.at[d, k - 1, a], z_rs.at[d, k - 1, a], {"expert": to}).wait_recv()

    def comes(up, k):
        return z >= k if up else z + k < nz

    def goes(up, k):
        there = z + 1 < nz if up else z >= 1
        return jnp.logical_and(there, comes(up, k)) if k else there

    for a in range(2):
        for up in (True, False):
            pl.when(goes(up, 0))(z_copy(up, 0, a).start)

    def z_step(k):
        for a in range(2):
            for up in (True, False):

                def arrived(up=up, a=a):
                    z_arrived(up, k, a)
                    q_copy(up, k, a, True).start()

                pl.when(comes(up, k))(arrived)
                if k + 1 < nz:
                    pl.when(goes(up, k))(z_copy(up, k, a).start)

    def w_step(i):
        w_arrived(0, i)
        w_copy(2, i).start()
        w_arrived(1, i)
        w_copy(3, i).start()

    for i in range(3):
        w_buf[i, s] = own[i][...]
    router[...] = jnp.zeros_like(router)
    router[: router_ref.shape[0], :] = router_ref[...]
    z_step(1)
    z_step(2)
    for i in range(3):
        w_step(i)
    z_step(3)
    for k in range(1, nz):
        for a in range(2):
            for up in (True, False):
                pl.when(comes(up, k))(q_copy(up, k, a, False).wait_recv)

    lane = lax.broadcasted_iota(jnp.int32, (nz * half, LANES), 1).astype(F32)
    me = z.astype(F32)
    for h in range(2):
        logits = dot(x_buf[h, :, :, :width].reshape(nz * half, width), router[...], ((1,), (1,)))
        meta = x_buf[h, :, :, width:].reshape(nz * half, LANES).astype(F32)
        first, second = meta[:, 0:1], meta[:, 1:2]
        hot0 = jnp.where(lane == first, 1.0, 0.0)
        hot1 = jnp.where(lane == second, 1.0, 0.0)
        gap = jnp.sum(logits * (hot0 - hot1), axis=1, keepdims=True)
        leading = jax.nn.sigmoid(gap)
        rest = 1.0 - leading
        mixing = jnp.where(first == me, leading, jnp.where(second == me, rest, 0.0))
        mix_buf[h] = mixing.astype(BF16).astype(F32)
        sign = jnp.where(first == me, 1.0, jnp.where(second == me, -1.0, 0.0))
        turn_buf[h] = (leading * rest * sign) * (hot0 - hot1)

    def accumulate(owner, start, which=(0, 1, 2)):
        cols = pl.ds(pl.multiple_of(owner * depth, depth), depth)
        for h in range(2):
            x = x_buf[h, :, :, cols].reshape(nz * half, depth)
            c = c_buf[h, :, :, cols].reshape(nz * half, depth)
            for i in which:
                term = dot(c if i == 2 else x, w_buf[i, owner])
                acc[i, h] = term if start else acc[i, h] + term

    accumulate(s, True)
    accumulate(x_nb, False)
    accumulate(y_nb, False)
    for i in range(3):
        w_arrived(2, i)
        w_arrived(3, i)
        accumulate(diag, False, (i,))

    step = 64

    @pl.loop(0, nz * half // step)
    def _(n):
        part = pl.ds(pl.multiple_of(n * step, step), step)
        for h in range(2):
            gate, up, cot_down = acc[0, h, part], acc[1, h, part], acc[2, h, part]
            sigma = jax.nn.sigmoid(gate)
            activ = gate * sigma
            slope = sigma * (1.0 + gate * (1.0 - sigma))
            hidden = (activ * up).astype(BF16).astype(F32)
            mix_part = jnp.sum(hidden * cot_down, axis=1, keepdims=True)
            grad = mix_buf[h, part] * cot_down
            joined[0, h, part] = (grad * up * slope).astype(BF16)
            joined[1, h, part] = (grad * activ).astype(BF16)
            coef = mix_part * turn_buf[h, part]
            high = coef.astype(BF16)
            coef_hi[h, part] = high
            coef_lo[h, part] = (coef - high.astype(F32)).astype(BF16)

    low, high = pl.ds(0, depth // 2), pl.ds(depth // 2, depth // 2)

    def weight_grad(owner, keep):
        cols = pl.ds(pl.multiple_of(owner * depth, depth), depth)
        for i in range(2):
            total = None
            for h in range(2):
                x = x_buf[h, :, :, cols].reshape(nz * half, depth)
                term = dot(x, joined[i, h], ((0,), (0,)))
                total = term if total is None else total + term
            keep[i] = total.astype(BF16)

    def g_copy(stage):
        to_x = stage % 2 == 0
        slot = 2 if stage < 2 else 0 if to_x else 1
        part = low if stage in (0, 2, 5) else high
        src = wgrad_send.at[slot, :, part]
        if stage < 2:
            dst = wgrad_recv.at[2, :, part]
        else:
            dst = wgrad_recv.at[0 if to_x else 1, :, part]
        return copy(src, dst, g_ss.at[stage], g_rs.at[stage], {"dp": x_nb if to_x else y_nb})

    weight_grad(diag, wgrad_send.at[2])
    g_copy(0).start()
    g_copy(1).start()
    weight_grad(x_nb, wgrad_send.at[0])
    g_copy(2).start()
    weight_grad(y_nb, wgrad_send.at[1])
    g_copy(3).start()

    def pass_on():
        g_copy(0).wait_recv()
        for i in range(2):
            mine = wgrad_send[1, i, low].astype(F32) + wgrad_recv[2, i, low].astype(F32)
            wgrad_send[1, i, low] = mine.astype(BF16)
        g_copy(5).start()
        g_copy(1).wait_recv()
        for i in range(2):
            mine = wgrad_send[0, i, high].astype(F32) + wgrad_recv[2, i, high].astype(F32)
            wgrad_send[0, i, high] = mine.astype(BF16)
        g_copy(4).start()

    def pick_grads(h, c):
        out = dot(joined[0, h], w_buf[0, c], ((1,), (1,))) + dot(joined[1, h], w_buf[1, c], ((1,), (1,)))
        part = router[:, c * depth : (c + 1) * depth]
        return out + dot(coef_hi[h], part) + dot(coef_lo[h], part)

    for c in range(4):
        pick_send[:, :, c * depth : (c + 1) * depth] = pick_grads(other, c).astype(BF16).reshape(nz, half, depth)
    p_copy = copy(pick_send, pick_recv, p_ss, p_rs, {"pair": other})
    p_copy.start()
    for c in range(4):
        pick_own[:, :, c * depth : (c + 1) * depth] = pick_grads(p, c).reshape(nz, half, depth)
    p_copy.wait_recv()

    def l_copy(j):
        to = lax.rem(z + j, nz)
        return copy(line_send.at[j - 1], line_recv.at[j - 1], l_ss.at[j - 1], l_rs.at[j - 1], {"expert": to})

    for j in range(1, nz):
        origin = lax.rem(z + j, nz)
        line_send[j - 1] = (pick_own[origin] + pick_recv[origin].astype(F32)).astype(BF16)
        l_copy(j).start()
    weight_grad(s, wgrad_send.at[3])
    pass_on()

    for j in range(1, nz):
        l_copy(j).wait_recv()
    total = pick_own[z] + pick_recv[z].astype(F32)
    for j in range(1, nz):
        total = total + line_recv[j - 1].astype(F32)
    fin_send[...] = total.astype(BF16)
    f_copy = copy(fin_send, fin_recv, f_ss, f_rs, {"pair": other})
    f_copy.start()
    row_out[pl.ds(pl.multiple_of(p * half, half), half), :] = fin_send[...]

    for stage in range(2, 6):
        g_copy(stage).wait_recv()
    for i, out in enumerate((gate_out, up_out)):
        sums = wgrad_send[3, i].astype(F32)
        for slot in range(2):
            sums = sums + wgrad_recv[slot, i].astype(F32)
        out[0] = sums.astype(BF16)
    f_copy.wait_recv()
    row_out[pl.ds(pl.multiple_of(other * half, half), half), :] = fin_recv[...]

    for i in range(3):
        for kind in range(4):
            w_copy(kind, i).wait_send()
    for a in range(2):
        for up in (True, False):
            for k in range(nz - 1):
                pl.when(goes(up, k))(z_copy(up, k, a).wait_send)
            for k in range(1, nz):
                pl.when(comes(up, k))(q_copy(up, k, a, True).wait_send)
    for stage in range(6):
        g_copy(stage).wait_send()
    p_copy.wait_send()
    for j in range(1, nz):
        l_copy(j).wait_send()
    f_copy.wait_send()


def dense(
    nz, byte_states, positions, picks, cotangent, router_weight, gate_weight, up_weight, down_weight
):
    rows, width = cotangent.shape
    half, depth, units = rows // 2, gate_weight.shape[1], gate_weight.shape[2]
    spots = positions[None, :]
    vmem, dma = pltpu.VMEM, pltpu.SemaphoreType.DMA
    whole = pl.BlockSpec(memory_space=vmem)
    scratch = [
        vmem((2, nz, half, width + LANES), BF16),
        vmem((2, nz, half, width), BF16),
        vmem((3, 4, depth, units), BF16),
        vmem((3, 2, nz * half, units), F32),
        vmem((2, 2, nz * half, units), BF16),
        vmem((2, nz * half, 1), F32),
        vmem((2, nz * half, LANES), F32),
        vmem((2, nz * half, LANES), BF16),
        vmem((2, nz * half, LANES), BF16),
        vmem((nz, half, width), BF16),
        vmem((nz, half, width), BF16),
        vmem((nz, half, width), F32),
        vmem((nz - 1, half, width), BF16),
        vmem((nz - 1, half, width), BF16),
        vmem((4, 2, depth, units), BF16),
        vmem((3, 2, depth, units), BF16),
        vmem((half, width), BF16),
        vmem((half, width), BF16),
        vmem((LANES, width), BF16),
        dma((4, 3)), dma((4, 3)),
        dma((2, nz - 1, 2)), dma((2, nz - 1, 2)),
        dma((2, nz - 1, 2)), dma((2, nz - 1, 2)),
        dma, dma,
        dma((nz - 1,)), dma((nz - 1,)),
        dma((6,)), dma((6,)),
        dma, dma,
    ]
    return pl.pallas_call(
        kernel,
        out_shape=(
            jax.ShapeDtypeStruct((rows, width), BF16),
            jax.ShapeDtypeStruct(gate_weight.shape, BF16),
            jax.ShapeDtypeStruct(up_weight.shape, BF16),
        ),
        in_specs=[whole] * 8,
        out_specs=(whole,) * 3,
        scratch_shapes=scratch,
        compiler_params=pltpu.CompilerParams(
            collective_id=0, has_side_effects=True, vmem_limit_bytes=52 * 2**20
        ),
    )(byte_states, spots, picks.T, cotangent, router_weight.T, gate_weight, up_weight, down_weight)


def local(
    byte_states, positions, picks, cotangent, router_weight, gate_weight, up_weight, down_weight
):
    byte_count = byte_states.shape[0]
    row_total = positions.shape[0]
    width = byte_states.shape[1]
    experts = router_weight.shape[1]
    top_count = picks.shape[1]
    capacity = max(2, 5 * row_total * top_count // (4 * experts))
    pick_total = row_total * top_count
    boundary = jnp.take(byte_states, positions % byte_count, axis=0)
    logits = jnp.dot(boundary, router_weight, preferred_element_type=jnp.float32)
    picked = jnp.take_along_axis(logits, picks, axis=1)
    leading = jax.nn.sigmoid(picked[:, 0] - picked[:, 1])
    mixing = jnp.stack([leading, 1.0 - leading], axis=1)
    mix_low = mixing.astype(jnp.bfloat16).reshape(-1)
    flat_picks = picks.reshape(-1)
    expert_ids = jnp.arange(experts, dtype=jnp.int32)
    one_hot = (flat_picks[:, None] == expert_ids[None, :]).astype(jnp.int32)
    order = jnp.arange(pick_total, dtype=jnp.int32)
    earlier = (order[None, :] < order[:, None]).astype(jnp.bfloat16)
    before = jnp.dot(earlier, one_hot.astype(jnp.bfloat16), preferred_element_type=jnp.float32)
    slot_rank = jnp.sum(before.astype(jnp.int32) * one_hot, axis=1)
    target = flat_picks * capacity + slot_rank
    slot_source = jnp.full((experts * capacity,), pick_total, jnp.int32)
    slot_source = slot_source.at[target].set(jnp.arange(pick_total, dtype=jnp.int32))
    is_live = slot_source < pick_total
    clamped = jnp.minimum(slot_source, pick_total - 1)
    source_row = clamped // top_count
    send_rows = jnp.where(is_live[:, None], boundary[source_row], 0).reshape(
        experts, capacity, width
    )
    send_cot = jnp.where(is_live[:, None], cotangent[source_row], 0).reshape(
        experts, capacity, width
    )
    send_mix = jnp.where(is_live, mix_low[clamped], 0).reshape(experts, capacity)
    gate_full, up_full, down_full = (
        lax.all_gather(gate_weight, "dp", axis=1, tiled=True),
        lax.all_gather(up_weight, "dp", axis=1, tiled=True),
        lax.all_gather(down_weight, "dp", axis=1, tiled=True),
    )
    hidden_half = gate_full.shape[2]
    gate_up = jnp.concatenate([gate_full[0], up_full[0]], axis=1)
    down_mat = down_full[0]
    recv_rows, recv_cot, recv_mix = (
        lax.all_to_all(send_rows, "expert", split_axis=0, concat_axis=0, tiled=True),
        lax.all_to_all(send_cot, "expert", split_axis=0, concat_axis=0, tiled=True),
        lax.all_to_all(send_mix, "expert", split_axis=0, concat_axis=0, tiled=True),
    )
    sources = recv_rows.shape[0]
    slot_total = sources * capacity
    expert_rows = recv_rows.reshape(slot_total, width)
    expert_cot = recv_cot.reshape(slot_total, width)
    expert_mix = recv_mix.reshape(slot_total)
    both_pre = jnp.dot(expert_rows, gate_up, preferred_element_type=jnp.float32)
    gate_pre = both_pre[:, :hidden_half]
    up_pre = both_pre[:, hidden_half:]
    sigma = jax.nn.sigmoid(gate_pre)
    activ = gate_pre * sigma
    slope = sigma * (1.0 + gate_pre * (1.0 - sigma))
    hidden = (activ * up_pre).astype(jnp.bfloat16)
    cot_down = jnp.dot(expert_cot, down_mat, preferred_element_type=jnp.float32)
    mix_part = jnp.sum(hidden.astype(jnp.float32) * cot_down, axis=1)
    scaled = (expert_mix.astype(jnp.float32)[:, None] * expert_cot.astype(jnp.float32)).astype(
        jnp.bfloat16
    )
    hidden_grad = jnp.dot(scaled, down_mat, preferred_element_type=jnp.float32)
    gate_pre_grad = (hidden_grad * up_pre * slope).astype(jnp.bfloat16)
    up_pre_grad = (hidden_grad * activ).astype(jnp.bfloat16)
    joined = jnp.concatenate([gate_pre_grad, up_pre_grad], axis=1)
    grad_part = lax.dot_general(
        joined, gate_up, (((1,), (1,)), ((), ())), preferred_element_type=jnp.float32
    )
    weight_sum = lax.psum_scatter(
        lax.dot_general(
            expert_rows, joined, (((0,), (0,)), ((), ())), preferred_element_type=jnp.float32
        ).astype(jnp.bfloat16),
        "dp",
        scatter_dimension=0,
        tiled=True,
    ).astype(jnp.float32)
    gate_grad = weight_sum[:, :hidden_half].astype(jnp.bfloat16)[None]
    up_grad = weight_sum[:, hidden_half:].astype(jnp.bfloat16)[None]
    grad_sum, mix_sum = (
        lax.psum(grad_part.astype(jnp.bfloat16), "pair").astype(jnp.float32),
        lax.psum(mix_part.astype(jnp.bfloat16), "pair").astype(jnp.float32),
    )
    grad_low = grad_sum.astype(jnp.bfloat16).reshape(sources, capacity, width)
    mix_grad_low = mix_sum.astype(jnp.bfloat16).reshape(sources, capacity)
    back_grad, back_mix = (
        lax.all_to_all(grad_low, "expert", split_axis=0, concat_axis=0, tiled=True),
        lax.all_to_all(mix_grad_low, "expert", split_axis=0, concat_axis=0, tiled=True),
    )
    pick_grad = back_grad.reshape(experts * capacity, width)[target]
    row_sum = jnp.sum(pick_grad.reshape(row_total, top_count, width).astype(jnp.float32), axis=1)
    mix_grad = (
        back_mix.reshape(experts * capacity)[target]
        .reshape(row_total, top_count)
        .astype(jnp.float32)
    )
    blended = jnp.sum(mixing * mix_grad, axis=1, keepdims=True)
    logit_grad = mixing * (mix_grad - blended)
    pick_hot = one_hot.reshape(row_total, top_count, experts).astype(jnp.float32)
    coeffs = jnp.sum(logit_grad[:, :, None] * pick_hot, axis=1)
    router_term = jnp.dot(
        coeffs, router_weight.astype(jnp.float32).T, precision=lax.Precision.HIGHEST
    )
    row_grad = (row_sum + router_term).astype(jnp.bfloat16)
    return (row_grad, gate_grad, up_grad)


def solution(mesh):
    in_specs = (
        P(("expert", "dp"), None),
        P(("expert", "dp")),
        P(("expert", "dp"), None),
        P(("expert", "dp"), None),
        P(),
        P("expert", "dp", "pair"),
        P("expert", "dp", "pair"),
        P("expert", "dp", "pair"),
    )
    out_specs = (P(("expert", "dp"), None), P("expert", "dp", "pair"), P("expert", "dp", "pair"))
    few = dict(mesh.shape) == {"expert": 4, "dp": 4, "pair": 2}
    body = functools.partial(dense, 4) if few else local
    return jax.shard_map(body, mesh=mesh, in_specs=in_specs, out_specs=out_specs, check_vma=False)
```

```python
import functools

import jax
import jax.numpy as jnp
from jax import lax
from jax.experimental import pallas as pl
from jax.experimental.pallas import tpu as pltpu
from jax.sharding import PartitionSpec as P

MESH = pl.DeviceIdType.MESH
LANES = 128
BF16, F32 = jnp.bfloat16, jnp.float32


def dot(a, b, contract=((1,), (0,))):
    return lax.dot_general(a, b, (contract, ((), ())), preferred_element_type=F32)


def kernel(
    byte_ref, pos_ref, pick_ref, cot_ref, router_ref, gate_ref, up_ref, down_ref,
    row_out, gate_out, up_out,
    x_buf, c_buf, w_buf, acc, joined, mix_buf, turn_buf, coef_hi, coef_lo,
    pick_send, pick_recv, pick_own, line_send, line_recv, wgrad_send, wgrad_recv, fin_send, fin_recv, router, byte_buf, hid_buf,
    w_ss, w_rs, z_ss, z_rs, q_ss, q_rs, p_ss, p_rs, l_ss, l_rs, g_ss, g_rs, f_ss, f_rs, o_s,
):
    z, s, p = lax.axis_index("expert"), lax.axis_index("dp"), lax.axis_index("pair")
    nz, half, width = x_buf.shape[1], x_buf.shape[2], c_buf.shape[3]
    depth = gate_ref.shape[1]
    other = 1 - p
    x_nb = s + 1 - 2 * lax.rem(s, 2)
    y_nb = lax.rem(s + 2, 4)
    diag = 3 - s

    def copy(src, dst, ss, rs, device):
        return pltpu.make_async_remote_copy(
            src_ref=src, dst_ref=dst, send_sem=ss, recv_sem=rs, device_id=device, device_id_type=MESH
        )

    barrier = pltpu.get_barrier_semaphore()
    peers = [{"dp": x_nb}, {"dp": y_nb}, {"dp": diag}, {"pair": other}]
    peers += [{"expert": lax.rem(z + j, nz)} for j in range(1, nz)]
    for peer in peers:
        pl.semaphore_signal(barrier, inc=1, device_id=peer, device_id_type=MESH)

    own = [gate_ref.at[0], up_ref.at[0], down_ref.at[0]]
    local_copies = [
        pltpu.make_async_copy(cot_ref.at[pl.ds(h * half, half)], c_buf.at[h, z], o_s.at[h]) for h in range(2)
    ]
    local_copies += [pltpu.make_async_copy(byte_ref, byte_buf, o_s.at[2])]
    local_copies += [pltpu.make_async_copy(own[i], w_buf.at[i, s], o_s.at[3 + i]) for i in range(3)]
    for one in local_copies:
        one.start()
    pl.semaphore_wait(barrier, len(peers))

    def w_copy(kind, i):
        if kind == 0:
            return copy(own[i], w_buf.at[i, s], w_ss.at[0, i], w_rs.at[0, i], {"dp": x_nb})
        if kind == 1:
            return copy(own[i], w_buf.at[i, s], w_ss.at[1, i], w_rs.at[1, i], {"dp": y_nb})
        part = pl.ds(0 if kind == 2 else depth // 2, depth // 2)
        frm, to = (x_nb, y_nb) if kind == 2 else (y_nb, x_nb)
        view = w_buf.at[i, frm, part]
        return copy(view, view, w_ss.at[kind, i], w_rs.at[kind, i], {"dp": to})

    def w_arrived(kind, i):
        frm = (x_nb, y_nb, diag, diag)[kind]
        view = w_buf.at[i, frm]
        if kind >= 2:
            view = w_buf.at[i, frm, pl.ds(0 if kind == 2 else depth // 2, depth // 2)]
        copy(view, view, w_ss.at[kind, i], w_rs.at[kind, i], {"dp": x_nb}).wait_recv()

    for i in range(3):
        w_copy(0, i).start()
        w_copy(1, i).start()

    bufs = (c_buf, x_buf)

    def z_copy(up, k, a):
        origin = lax.rem(z + (nz - k if up else k), nz)
        view = bufs[a].at[p, origin]
        d = 0 if up else 1
        to = lax.rem(z + (1 if up else nz - 1), nz)
        return copy(view, view, z_ss.at[d, k, a], z_rs.at[d, k, a], {"expert": to})

    def q_copy(up, k, a, mine):
        origin = lax.rem(z + (nz - k if up else k), nz)
        view = bufs[a].at[p if mine else other, origin]
        d = 0 if up else 1
        return copy(view, view, q_ss.at[d, k - 1, a], q_rs.at[d, k - 1, a], {"pair": other})

    def z_arrived(up, k, a):
        origin = lax.rem(z + (nz - k if up else k), nz)
        view = bufs[a].at[p, origin]
        d = 0 if up else 1
        to = lax.rem(z + 1, nz)
        copy(view, view, z_ss.at[d, k - 1, a], z_rs.at[d, k - 1, a], {"expert": to}).wait_recv()

    def comes(up, k):
        return z >= k if up else z + k < nz

    def goes(up, k):
        there = z + 1 < nz if up else z >= 1
        return jnp.logical_and(there, comes(up, k)) if k else there

    for one in local_copies[:2]:
        one.wait()
    for up in (True, False):
        pl.when(goes(up, 0))(z_copy(up, 0, 0).start)

    local_copies[2].wait()
    count = byte_buf.shape[0]
    spots = lax.broadcasted_iota(jnp.int32, (count, 2 * half), 0) + (z * 4 + s) * count
    hot = jnp.where(spots == pos_ref[...], 1.0, 0.0).astype(BF16)
    for c in range(0, width, depth):
        rows = dot(hot, byte_buf[:, c : c + depth], ((0,), (0,))).astype(BF16)
        for h in range(2):
            x_buf[h, z, :, c : c + depth] = rows[h * half : (h + 1) * half]
    place = lax.broadcasted_iota(jnp.int32, (LANES, 2 * half), 0)
    picked = pick_ref[...].astype(F32)
    meta = jnp.where(place == 0, picked[0:1, :], jnp.where(place == 1, picked[1:2, :], 0.0)).T
    for h in range(2):
        x_buf[h, z, :, width:] = meta[h * half : (h + 1) * half].astype(BF16)
    for up in (True, False):
        pl.when(goes(up, 0))(z_copy(up, 0, 1).start)

    def z_step(k):
        for a in range(2):
            for up in (True, False):

                def arrived(up=up, a=a):
                    z_arrived(up, k, a)
                    q_copy(up, k, a, True).start()

                pl.when(comes(up, k))(arrived)
                if k + 1 < nz:
                    pl.when(goes(up, k))(z_copy(up, k, a).start)

    def w_step(i):
        w_arrived(0, i)
        w_copy(2, i).start()
        w_arrived(1, i)
        w_copy(3, i).start()

    for one in local_copies[3:]:
        one.wait()
    router[...] = jnp.zeros_like(router)
    router[: router_ref.shape[0], :] = router_ref[...]
    z_step(1)
    z_step(2)
    for i in range(3):
        w_step(i)
    z_step(3)
    for k in range(1, nz):
        for a in range(2):
            for up in (True, False):
                pl.when(comes(up, k))(q_copy(up, k, a, False).wait_recv)

    lane = lax.broadcasted_iota(jnp.int32, (nz * half, LANES), 1).astype(F32)
    me = z.astype(F32)
    for h in range(2):
        logits = dot(x_buf[h, :, :, :width].reshape(nz * half, width), router[...], ((1,), (1,)))
        meta = x_buf[h, :, :, width:].reshape(nz * half, LANES).astype(F32)
        first, second = meta[:, 0:1], meta[:, 1:2]
        hot0 = jnp.where(lane == first, 1.0, 0.0)
        hot1 = jnp.where(lane == second, 1.0, 0.0)
        gap = jnp.sum(logits * (hot0 - hot1), axis=1, keepdims=True)
        leading = jax.nn.sigmoid(gap)
        rest = 1.0 - leading
        mixing = jnp.where(first == me, leading, jnp.where(second == me, rest, 0.0))
        mix_buf[h] = mixing.astype(BF16).astype(F32)
        sign = jnp.where(first == me, 1.0, jnp.where(second == me, -1.0, 0.0))
        turn_buf[h] = (leading * rest * sign) * (hot0 - hot1)

    def accumulate(owner, start, which=(0, 1, 2)):
        cols = pl.ds(pl.multiple_of(owner * depth, depth), depth)
        for h in range(2):
            x = x_buf[h, :, :, cols].reshape(nz * half, depth)
            c = c_buf[h, :, :, cols].reshape(nz * half, depth)
            for i in which:
                term = dot(c if i == 2 else x, w_buf[i, owner])
                acc[i, h] = term if start else acc[i, h] + term

    accumulate(s, True)
    accumulate(x_nb, False)
    accumulate(y_nb, False)
    for i in range(2):
        w_arrived(2, i)
        w_arrived(3, i)
        accumulate(diag, False, (i,))

    step = 64

    @pl.loop(0, nz * half // step)
    def _(n):
        part = pl.ds(pl.multiple_of(n * step, step), step)
        for h in range(2):
            gate, up = acc[0, h, part], acc[1, h, part]
            sigma = jax.nn.sigmoid(gate)
            activ = gate * sigma
            slope = sigma * (1.0 + gate * (1.0 - sigma))
            hid_buf[h, part] = (activ * up).astype(BF16)
            acc[0, h, part] = mix_buf[h, part] * (up * slope)
            acc[1, h, part] = mix_buf[h, part] * activ

    w_arrived(2, 2)
    w_arrived(3, 2)
    accumulate(diag, False, (2,))

    @pl.loop(0, nz * half // step)
    def _(n):
        part = pl.ds(pl.multiple_of(n * step, step), step)
        for h in range(2):
            cot_down = acc[2, h, part]
            joined[0, h, part] = (cot_down * acc[0, h, part]).astype(BF16)
            joined[1, h, part] = (cot_down * acc[1, h, part]).astype(BF16)

    low, high = pl.ds(0, depth // 2), pl.ds(depth // 2, depth // 2)

    def weight_grad(owner, keep):
        cols = pl.ds(pl.multiple_of(owner * depth, depth), depth)
        for i in range(2):
            total = None
            for h in range(2):
                x = x_buf[h, :, :, cols].reshape(nz * half, depth)
                term = dot(x, joined[i, h], ((0,), (0,)))
                total = term if total is None else total + term
            keep[i] = total.astype(BF16)

    def g_copy(stage):
        to_x = stage % 2 == 0
        slot = 2 if stage < 2 else 0 if to_x else 1
        part = low if stage in (0, 2, 5) else high
        src = wgrad_send.at[slot, :, part]
        if stage < 2:
            dst = wgrad_recv.at[2, :, part]
        else:
            dst = wgrad_recv.at[0 if to_x else 1, :, part]
        return copy(src, dst, g_ss.at[stage], g_rs.at[stage], {"dp": x_nb if to_x else y_nb})

    weight_grad(diag, wgrad_send.at[2])
    g_copy(0).start()
    g_copy(1).start()
    weight_grad(x_nb, wgrad_send.at[0])
    g_copy(2).start()
    weight_grad(y_nb, wgrad_send.at[1])
    g_copy(3).start()

    def pass_on():
        g_copy(0).wait_recv()
        for i in range(2):
            mine = wgrad_send[1, i, low].astype(F32) + wgrad_recv[2, i, low].astype(F32)
            wgrad_send[1, i, low] = mine.astype(BF16)
        g_copy(5).start()
        g_copy(1).wait_recv()
        for i in range(2):
            mine = wgrad_send[0, i, high].astype(F32) + wgrad_recv[2, i, high].astype(F32)
            wgrad_send[0, i, high] = mine.astype(BF16)
        g_copy(4).start()

    @pl.loop(0, nz * half // step)
    def _(n):
        part = pl.ds(pl.multiple_of(n * step, step), step)
        for h in range(2):
            mix_part = jnp.sum(hid_buf[h, part].astype(F32) * acc[2, h, part], axis=1, keepdims=True)
            coef = mix_part * turn_buf[h, part]
            top = coef.astype(BF16)
            coef_hi[h, part] = top
            coef_lo[h, part] = (coef - top.astype(F32)).astype(BF16)

    def pick_grads(h, c):
        out = dot(joined[0, h], w_buf[0, c], ((1,), (1,))) + dot(joined[1, h], w_buf[1, c], ((1,), (1,)))
        part = router[:, c * depth : (c + 1) * depth]
        return out + dot(coef_hi[h], part) + dot(coef_lo[h], part)

    for c in range(4):
        pick_send[:, :, c * depth : (c + 1) * depth] = pick_grads(other, c).astype(BF16).reshape(nz, half, depth)
    p_copy = copy(pick_send, pick_recv, p_ss, p_rs, {"pair": other})
    p_copy.start()
    for c in range(4):
        pick_own[:, :, c * depth : (c + 1) * depth] = pick_grads(p, c).reshape(nz, half, depth)
    p_copy.wait_recv()

    def l_copy(j):
        to = lax.rem(z + j, nz)
        return copy(line_send.at[j - 1], line_recv.at[j - 1], l_ss.at[j - 1], l_rs.at[j - 1], {"expert": to})

    for j in range(1, nz):
        origin = lax.rem(z + j, nz)
        line_send[j - 1] = (pick_own[origin] + pick_recv[origin].astype(F32)).astype(BF16)
        l_copy(j).start()
    weight_grad(s, wgrad_send.at[3])
    pass_on()

    for j in range(1, nz):
        l_copy(j).wait_recv()
    total = pick_own[z] + pick_recv[z].astype(F32)
    for j in range(1, nz):
        total = total + line_recv[j - 1].astype(F32)
    fin_send[...] = total.astype(BF16)
    f_copy = copy(fin_send, fin_recv, f_ss, f_rs, {"pair": other})
    f_copy.start()
    row_out[pl.ds(pl.multiple_of(p * half, half), half), :] = fin_send[...]

    for stage in range(2, 6):
        g_copy(stage).wait_recv()
    for i, out in enumerate((gate_out, up_out)):
        sums = wgrad_send[3, i].astype(F32)
        for slot in range(2):
            sums = sums + wgrad_recv[slot, i].astype(F32)
        out[0] = sums.astype(BF16)
    f_copy.wait_recv()
    row_out[pl.ds(pl.multiple_of(other * half, half), half), :] = fin_recv[...]

    for i in range(3):
        for kind in range(4):
            w_copy(kind, i).wait_send()
    for a in range(2):
        for up in (True, False):
            for k in range(nz - 1):
                pl.when(goes(up, k))(z_copy(up, k, a).wait_send)
            for k in range(1, nz):
                pl.when(comes(up, k))(q_copy(up, k, a, True).wait_send)
    for stage in range(6):
        g_copy(stage).wait_send()
    p_copy.wait_send()
    for j in range(1, nz):
        l_copy(j).wait_send()
    f_copy.wait_send()


def dense(
    nz, byte_states, positions, picks, cotangent, router_weight, gate_weight, up_weight, down_weight
):
    rows, width = cotangent.shape
    half, depth, units = rows // 2, gate_weight.shape[1], gate_weight.shape[2]
    spots = positions[None, :]
    vmem, dma = pltpu.VMEM, pltpu.SemaphoreType.DMA
    whole, far = pl.BlockSpec(memory_space=vmem), pl.BlockSpec(memory_space=pl.ANY)
    scratch = [
        vmem((2, nz, half, width + LANES), BF16),
        vmem((2, nz, half, width), BF16),
        vmem((3, 4, depth, units), BF16),
        vmem((3, 2, nz * half, units), F32),
        vmem((2, 2, nz * half, units), BF16),
        vmem((2, nz * half, 1), F32),
        vmem((2, nz * half, LANES), F32),
        vmem((2, nz * half, LANES), BF16),
        vmem((2, nz * half, LANES), BF16),
        vmem((nz, half, width), BF16),
        vmem((nz, half, width), BF16),
        vmem((nz, half, width), F32),
        vmem((nz - 1, half, width), BF16),
        vmem((nz - 1, half, width), BF16),
        vmem((4, 2, depth, units), BF16),
        vmem((3, 2, depth, units), BF16),
        vmem((half, width), BF16),
        vmem((half, width), BF16),
        vmem((LANES, width), BF16),
        vmem(byte_states.shape, BF16),
        vmem((2, nz * half, units), BF16),
        dma((4, 3)), dma((4, 3)),
        dma((2, nz - 1, 2)), dma((2, nz - 1, 2)),
        dma((2, nz - 1, 2)), dma((2, nz - 1, 2)),
        dma, dma,
        dma((nz - 1,)), dma((nz - 1,)),
        dma((6,)), dma((6,)),
        dma, dma,
        dma((6,)),
    ]
    return pl.pallas_call(
        kernel,
        out_shape=(
            jax.ShapeDtypeStruct((rows, width), BF16),
            jax.ShapeDtypeStruct(gate_weight.shape, BF16),
            jax.ShapeDtypeStruct(up_weight.shape, BF16),
        ),
        in_specs=[far, whole, whole, far, whole, far, far, far],
        out_specs=(whole,) * 3,
        scratch_shapes=scratch,
        compiler_params=pltpu.CompilerParams(
            collective_id=0, has_side_effects=True, vmem_limit_bytes=58 * 2**20
        ),
    )(byte_states, spots, picks.T, cotangent, router_weight.T, gate_weight, up_weight, down_weight)


def local(
    byte_states, positions, picks, cotangent, router_weight, gate_weight, up_weight, down_weight
):
    byte_count = byte_states.shape[0]
    row_total = positions.shape[0]
    width = byte_states.shape[1]
    experts = router_weight.shape[1]
    top_count = picks.shape[1]
    capacity = max(2, 5 * row_total * top_count // (4 * experts))
    pick_total = row_total * top_count
    boundary = jnp.take(byte_states, positions % byte_count, axis=0)
    logits = jnp.dot(boundary, router_weight, preferred_element_type=jnp.float32)
    picked = jnp.take_along_axis(logits, picks, axis=1)
    leading = jax.nn.sigmoid(picked[:, 0] - picked[:, 1])
    mixing = jnp.stack([leading, 1.0 - leading], axis=1)
    mix_low = mixing.astype(jnp.bfloat16).reshape(-1)
    flat_picks = picks.reshape(-1)
    expert_ids = jnp.arange(experts, dtype=jnp.int32)
    one_hot = (flat_picks[:, None] == expert_ids[None, :]).astype(jnp.int32)
    order = jnp.arange(pick_total, dtype=jnp.int32)
    earlier = (order[None, :] < order[:, None]).astype(jnp.bfloat16)
    before = jnp.dot(earlier, one_hot.astype(jnp.bfloat16), preferred_element_type=jnp.float32)
    slot_rank = jnp.sum(before.astype(jnp.int32) * one_hot, axis=1)
    target = flat_picks * capacity + slot_rank
    slot_source = jnp.full((experts * capacity,), pick_total, jnp.int32)
    slot_source = slot_source.at[target].set(jnp.arange(pick_total, dtype=jnp.int32))
    is_live = slot_source < pick_total
    clamped = jnp.minimum(slot_source, pick_total - 1)
    source_row = clamped // top_count
    send_rows = jnp.where(is_live[:, None], boundary[source_row], 0).reshape(
        experts, capacity, width
    )
    send_cot = jnp.where(is_live[:, None], cotangent[source_row], 0).reshape(
        experts, capacity, width
    )
    send_mix = jnp.where(is_live, mix_low[clamped], 0).reshape(experts, capacity)
    gate_full, up_full, down_full = (
        lax.all_gather(gate_weight, "dp", axis=1, tiled=True),
        lax.all_gather(up_weight, "dp", axis=1, tiled=True),
        lax.all_gather(down_weight, "dp", axis=1, tiled=True),
    )
    hidden_half = gate_full.shape[2]
    gate_up = jnp.concatenate([gate_full[0], up_full[0]], axis=1)
    down_mat = down_full[0]
    recv_rows, recv_cot, recv_mix = (
        lax.all_to_all(send_rows, "expert", split_axis=0, concat_axis=0, tiled=True),
        lax.all_to_all(send_cot, "expert", split_axis=0, concat_axis=0, tiled=True),
        lax.all_to_all(send_mix, "expert", split_axis=0, concat_axis=0, tiled=True),
    )
    sources = recv_rows.shape[0]
    slot_total = sources * capacity
    expert_rows = recv_rows.reshape(slot_total, width)
    expert_cot = recv_cot.reshape(slot_total, width)
    expert_mix = recv_mix.reshape(slot_total)
    both_pre = jnp.dot(expert_rows, gate_up, preferred_element_type=jnp.float32)
    gate_pre = both_pre[:, :hidden_half]
    up_pre = both_pre[:, hidden_half:]
    sigma = jax.nn.sigmoid(gate_pre)
    activ = gate_pre * sigma
    slope = sigma * (1.0 + gate_pre * (1.0 - sigma))
    hidden = (activ * up_pre).astype(jnp.bfloat16)
    cot_down = jnp.dot(expert_cot, down_mat, preferred_element_type=jnp.float32)
    mix_part = jnp.sum(hidden.astype(jnp.float32) * cot_down, axis=1)
    scaled = (expert_mix.astype(jnp.float32)[:, None] * expert_cot.astype(jnp.float32)).astype(
        jnp.bfloat16
    )
    hidden_grad = jnp.dot(scaled, down_mat, preferred_element_type=jnp.float32)
    gate_pre_grad = (hidden_grad * up_pre * slope).astype(jnp.bfloat16)
    up_pre_grad = (hidden_grad * activ).astype(jnp.bfloat16)
    joined = jnp.concatenate([gate_pre_grad, up_pre_grad], axis=1)
    grad_part = lax.dot_general(
        joined, gate_up, (((1,), (1,)), ((), ())), preferred_element_type=jnp.float32
    )
    weight_sum = lax.psum_scatter(
        lax.dot_general(
            expert_rows, joined, (((0,), (0,)), ((), ())), preferred_element_type=jnp.float32
        ).astype(jnp.bfloat16),
        "dp",
        scatter_dimension=0,
        tiled=True,
    ).astype(jnp.float32)
    gate_grad = weight_sum[:, :hidden_half].astype(jnp.bfloat16)[None]
    up_grad = weight_sum[:, hidden_half:].astype(jnp.bfloat16)[None]
    grad_sum, mix_sum = (
        lax.psum(grad_part.astype(jnp.bfloat16), "pair").astype(jnp.float32),
        lax.psum(mix_part.astype(jnp.bfloat16), "pair").astype(jnp.float32),
    )
    grad_low = grad_sum.astype(jnp.bfloat16).reshape(sources, capacity, width)
    mix_grad_low = mix_sum.astype(jnp.bfloat16).reshape(sources, capacity)
    back_grad, back_mix = (
        lax.all_to_all(grad_low, "expert", split_axis=0, concat_axis=0, tiled=True),
        lax.all_to_all(mix_grad_low, "expert", split_axis=0, concat_axis=0, tiled=True),
    )
    pick_grad = back_grad.reshape(experts * capacity, width)[target]
    row_sum = jnp.sum(pick_grad.reshape(row_total, top_count, width).astype(jnp.float32), axis=1)
    mix_grad = (
        back_mix.reshape(experts * capacity)[target]
        .reshape(row_total, top_count)
        .astype(jnp.float32)
    )
    blended = jnp.sum(mixing * mix_grad, axis=1, keepdims=True)
    logit_grad = mixing * (mix_grad - blended)
    pick_hot = one_hot.reshape(row_total, top_count, experts).astype(jnp.float32)
    coeffs = jnp.sum(logit_grad[:, :, None] * pick_hot, axis=1)
    router_term = jnp.dot(
        coeffs, router_weight.astype(jnp.float32).T, precision=lax.Precision.HIGHEST
    )
    row_grad = (row_sum + router_term).astype(jnp.bfloat16)
    return (row_grad, gate_grad, up_grad)


def solution(mesh):
    in_specs = (
        P(("expert", "dp"), None),
        P(("expert", "dp")),
        P(("expert", "dp"), None),
        P(("expert", "dp"), None),
        P(),
        P("expert", "dp", "pair"),
        P("expert", "dp", "pair"),
        P("expert", "dp", "pair"),
    )
    out_specs = (P(("expert", "dp"), None), P("expert", "dp", "pair"), P("expert", "dp", "pair"))
    few = dict(mesh.shape) == {"expert": 4, "dp": 4, "pair": 2}
    body = functools.partial(dense, 4) if few else local
    return jax.shard_map(body, mesh=mesh, in_specs=in_specs, out_specs=out_specs, check_vma=False)
```

```python
import functools

import jax
import jax.numpy as jnp
from jax import lax
from jax.experimental import pallas as pl
from jax.experimental.pallas import tpu as pltpu
from jax.sharding import PartitionSpec as P

MESH = pl.DeviceIdType.MESH
LANES = 128
BF16, F32 = jnp.bfloat16, jnp.float32


def dot(a, b, contract=((1,), (0,))):
    return lax.dot_general(a, b, (contract, ((), ())), preferred_element_type=F32)


def kernel(
    byte_ref, pos_ref, pick_ref, cot_ref, router_ref, gate_ref, up_ref, down_ref,
    row_out, gate_out, up_out,
    x_buf, c_buf, w_buf, acc, joined, mix_buf, turn_buf, coef_hi, coef_lo,
    pick_send, pick_recv, pick_own, line_send, line_recv, wgrad_send, wgrad_recv, fin_send, fin_recv, router, byte_buf, hid_buf,
    w_ss, w_rs, z_ss, z_rs, q_ss, q_rs, p_ss, p_rs, l_ss, l_rs, g_ss, g_rs, f_ss, f_rs, o_s,
):
    z, s, p = lax.axis_index("expert"), lax.axis_index("dp"), lax.axis_index("pair")
    nz, half, width = x_buf.shape[1], x_buf.shape[2], c_buf.shape[3]
    depth = gate_ref.shape[1]
    other = 1 - p
    x_nb = s + 1 - 2 * lax.rem(s, 2)
    y_nb = lax.rem(s + 2, 4)
    diag = 3 - s

    def copy(src, dst, ss, rs, device):
        return pltpu.make_async_remote_copy(
            src_ref=src, dst_ref=dst, send_sem=ss, recv_sem=rs, device_id=device, device_id_type=MESH
        )

    barrier = pltpu.get_barrier_semaphore()
    peers = [{"dp": x_nb}, {"dp": y_nb}, {"dp": diag}, {"pair": other}]
    peers += [{"expert": lax.rem(z + j, nz)} for j in range(1, nz)]
    for peer in peers:
        pl.semaphore_signal(barrier, inc=1, device_id=peer, device_id_type=MESH)

    own = [gate_ref.at[0], up_ref.at[0], down_ref.at[0]]
    local_copies = [
        pltpu.make_async_copy(cot_ref.at[pl.ds(h * half, half)], c_buf.at[h, z], o_s.at[h]) for h in range(2)
    ]
    local_copies += [pltpu.make_async_copy(byte_ref, byte_buf, o_s.at[2])]
    local_copies += [pltpu.make_async_copy(own[i], w_buf.at[i, s], o_s.at[3 + i]) for i in range(3)]
    for one in local_copies:
        one.start()
    pl.semaphore_wait(barrier, len(peers))

    def w_copy(kind, i):
        if kind == 0:
            return copy(own[i], w_buf.at[i, s], w_ss.at[0, i], w_rs.at[0, i], {"dp": x_nb})
        if kind == 1:
            return copy(own[i], w_buf.at[i, s], w_ss.at[1, i], w_rs.at[1, i], {"dp": y_nb})
        part = pl.ds(0 if kind == 2 else depth // 2, depth // 2)
        frm, to = (x_nb, y_nb) if kind == 2 else (y_nb, x_nb)
        view = w_buf.at[i, frm, part]
        return copy(view, view, w_ss.at[kind, i], w_rs.at[kind, i], {"dp": to})

    def w_arrived(kind, i):
        frm = (x_nb, y_nb, diag, diag)[kind]
        view = w_buf.at[i, frm]
        if kind >= 2:
            view = w_buf.at[i, frm, pl.ds(0 if kind == 2 else depth // 2, depth // 2)]
        copy(view, view, w_ss.at[kind, i], w_rs.at[kind, i], {"dp": x_nb}).wait_recv()

    for i in range(3):
        w_copy(0, i).start()
        w_copy(1, i).start()

    bufs = (c_buf, x_buf)

    def z_copy(up, k, a):
        origin = lax.rem(z + (nz - k if up else k), nz)
        view = bufs[a].at[p, origin]
        d = 0 if up else 1
        to = lax.rem(z + (1 if up else nz - 1), nz)
        return copy(view, view, z_ss.at[d, k, a], z_rs.at[d, k, a], {"expert": to})

    def q_copy(up, k, a, mine):
        origin = lax.rem(z + (nz - k if up else k), nz)
        view = bufs[a].at[p if mine else other, origin]
        d = 0 if up else 1
        return copy(view, view, q_ss.at[d, k - 1, a], q_rs.at[d, k - 1, a], {"pair": other})

    def z_arrived(up, k, a):
        origin = lax.rem(z + (nz - k if up else k), nz)
        view = bufs[a].at[p, origin]
        d = 0 if up else 1
        to = lax.rem(z + 1, nz)
        copy(view, view, z_ss.at[d, k - 1, a], z_rs.at[d, k - 1, a], {"expert": to}).wait_recv()

    def comes(up, k):
        return z >= k if up else z + k < nz

    def goes(up, k):
        there = z + 1 < nz if up else z >= 1
        return jnp.logical_and(there, comes(up, k)) if k else there

    for one in local_copies[:2]:
        one.wait()
    for up in (True, False):
        pl.when(goes(up, 0))(z_copy(up, 0, 0).start)

    local_copies[2].wait()
    count = byte_buf.shape[0]
    spots = lax.broadcasted_iota(jnp.int32, (count, 2 * half), 0) + (z * 4 + s) * count
    hot = jnp.where(spots == pos_ref[...], 1.0, 0.0).astype(BF16)
    for c in range(0, width, depth):
        rows = dot(hot, byte_buf[:, c : c + depth], ((0,), (0,))).astype(BF16)
        for h in range(2):
            x_buf[h, z, :, c : c + depth] = rows[h * half : (h + 1) * half]
    place = lax.broadcasted_iota(jnp.int32, (LANES, 2 * half), 0)
    picked = pick_ref[...].astype(F32)
    meta = jnp.where(place == 0, picked[0:1, :], jnp.where(place == 1, picked[1:2, :], 0.0)).T
    for h in range(2):
        x_buf[h, z, :, width:] = meta[h * half : (h + 1) * half].astype(BF16)
    for up in (True, False):
        pl.when(goes(up, 0))(z_copy(up, 0, 1).start)

    def z_step(k):
        for a in range(2):
            for up in (True, False):

                def arrived(up=up, a=a):
                    z_arrived(up, k, a)
                    q_copy(up, k, a, True).start()

                pl.when(comes(up, k))(arrived)
                if k + 1 < nz:
                    pl.when(goes(up, k))(z_copy(up, k, a).start)

    def w_step(i):
        w_arrived(0, i)
        w_copy(2, i).start()
        w_arrived(1, i)
        w_copy(3, i).start()

    for one in local_copies[3:]:
        one.wait()
    router[...] = jnp.zeros_like(router)
    router[: router_ref.shape[0], :] = router_ref[...]
    z_step(1)
    z_step(2)
    for i in range(3):
        w_step(i)
    z_step(3)
    for k in range(1, nz):
        for a in range(2):
            for up in (True, False):
                pl.when(comes(up, k))(q_copy(up, k, a, False).wait_recv)

    lane = lax.broadcasted_iota(jnp.int32, (nz * half, LANES), 1).astype(F32)
    me = z.astype(F32)
    for h in range(2):
        logits = dot(x_buf[h, :, :, :width].reshape(nz * half, width), router[...], ((1,), (1,)))
        meta = x_buf[h, :, :, width:].reshape(nz * half, LANES).astype(F32)
        first, second = meta[:, 0:1], meta[:, 1:2]
        hot0 = jnp.where(lane == first, 1.0, 0.0)
        hot1 = jnp.where(lane == second, 1.0, 0.0)
        gap = jnp.sum(logits * (hot0 - hot1), axis=1, keepdims=True)
        leading = jax.nn.sigmoid(gap)
        rest = 1.0 - leading
        mixing = jnp.where(first == me, leading, jnp.where(second == me, rest, 0.0))
        mix_buf[h] = mixing.astype(BF16).astype(F32)
        sign = jnp.where(first == me, 1.0, jnp.where(second == me, -1.0, 0.0))
        turn_buf[h] = (leading * rest * sign) * (hot0 - hot1)

    def accumulate(owner, start, which=(0, 1, 2)):
        cols = pl.ds(pl.multiple_of(owner * depth, depth), depth)
        for h in range(2):
            x = x_buf[h, :, :, cols].reshape(nz * half, depth)
            c = c_buf[h, :, :, cols].reshape(nz * half, depth)
            for i in which:
                term = dot(c if i == 2 else x, w_buf[i, owner])
                acc[i, h] = term if start else acc[i, h] + term

    accumulate(s, True)
    accumulate(x_nb, False)
    accumulate(y_nb, False)
    for i in range(2):
        w_arrived(2, i)
        w_arrived(3, i)
        accumulate(diag, False, (i,))

    step = 64

    @pl.loop(0, nz * half // step)
    def _(n):
        part = pl.ds(pl.multiple_of(n * step, step), step)
        for h in range(2):
            gate, up = acc[0, h, part], acc[1, h, part]
            sigma = jax.nn.sigmoid(gate)
            activ = gate * sigma
            slope = sigma * (1.0 + gate * (1.0 - sigma))
            hid_buf[h, part] = (activ * up).astype(BF16)
            acc[0, h, part] = mix_buf[h, part] * (up * slope)
            acc[1, h, part] = mix_buf[h, part] * activ

    w_arrived(2, 2)
    w_arrived(3, 2)
    accumulate(diag, False, (2,))

    @pl.loop(0, nz * half // step)
    def _(n):
        part = pl.ds(pl.multiple_of(n * step, step), step)
        for h in range(2):
            cot_down = acc[2, h, part]
            joined[0, h, part] = (cot_down * acc[0, h, part]).astype(BF16)
            joined[1, h, part] = (cot_down * acc[1, h, part]).astype(BF16)

    low, high = pl.ds(0, depth // 2), pl.ds(depth // 2, depth // 2)

    def weight_grad(owner, keep, stages=()):
        cols = pl.ds(pl.multiple_of(owner * depth, depth), depth)
        for i in range(2):
            total = None
            for h in range(2):
                x = x_buf[h, :, :, cols].reshape(nz * half, depth)
                term = dot(x, joined[i, h], ((0,), (0,)))
                total = term if total is None else total + term
            keep[i] = total.astype(BF16)
            for stage in stages:
                g_copy(stage, i).start()

    def g_copy(stage, i):
        to_x = stage % 2 == 0
        slot = 2 if stage < 2 else 0 if to_x else 1
        part = low if stage in (0, 2, 5) else high
        src = wgrad_send.at[slot, i, part]
        if stage < 2:
            dst = wgrad_recv.at[2, i, part]
        else:
            dst = wgrad_recv.at[0 if to_x else 1, i, part]
        return copy(src, dst, g_ss.at[stage, i], g_rs.at[stage, i], {"dp": x_nb if to_x else y_nb})

    weight_grad(diag, wgrad_send.at[2], (0, 1))
    weight_grad(x_nb, wgrad_send.at[0], (2,))
    weight_grad(y_nb, wgrad_send.at[1], (3,))

    def pass_on():
        for i in range(2):
            for came, slot, part, stage in ((0, 1, low, 5), (1, 0, high, 4)):
                g_copy(came, i).wait_recv()
                mine = wgrad_send[slot, i, part].astype(F32) + wgrad_recv[2, i, part].astype(F32)
                wgrad_send[slot, i, part] = mine.astype(BF16)
                g_copy(stage, i).start()

    @pl.loop(0, nz * half // step)
    def _(n):
        part = pl.ds(pl.multiple_of(n * step, step), step)
        for h in range(2):
            mix_part = jnp.sum(hid_buf[h, part].astype(F32) * acc[2, h, part], axis=1, keepdims=True)
            coef = mix_part * turn_buf[h, part]
            top = coef.astype(BF16)
            coef_hi[h, part] = top
            coef_lo[h, part] = (coef - top.astype(F32)).astype(BF16)

    def pick_grads(h, c):
        out = dot(joined[0, h], w_buf[0, c], ((1,), (1,))) + dot(joined[1, h], w_buf[1, c], ((1,), (1,)))
        part = router[:, c * depth : (c + 1) * depth]
        return out + dot(coef_hi[h], part) + dot(coef_lo[h], part)

    for c in range(4):
        pick_send[:, :, c * depth : (c + 1) * depth] = pick_grads(other, c).astype(BF16).reshape(nz, half, depth)
    p_copy = copy(pick_send, pick_recv, p_ss, p_rs, {"pair": other})
    p_copy.start()
    for c in range(4):
        pick_own[:, :, c * depth : (c + 1) * depth] = pick_grads(p, c).reshape(nz, half, depth)
    p_copy.wait_recv()

    def l_copy(j):
        to = lax.rem(z + j, nz)
        return copy(line_send.at[j - 1], line_recv.at[j - 1], l_ss.at[j - 1], l_rs.at[j - 1], {"expert": to})

    for j in range(1, nz):
        origin = lax.rem(z + j, nz)
        line_send[j - 1] = (pick_own[origin] + pick_recv[origin].astype(F32)).astype(BF16)
        l_copy(j).start()
    weight_grad(s, wgrad_send.at[3])
    pass_on()

    for j in range(1, nz):
        l_copy(j).wait_recv()
    total = pick_own[z] + pick_recv[z].astype(F32)
    for j in range(1, nz):
        total = total + line_recv[j - 1].astype(F32)
    fin_send[...] = total.astype(BF16)
    f_copy = copy(fin_send, fin_recv, f_ss, f_rs, {"pair": other})
    f_copy.start()
    row_out[pl.ds(pl.multiple_of(p * half, half), half), :] = fin_send[...]

    for stage in range(2, 6):
        for i in range(2):
            g_copy(stage, i).wait_recv()
    for i, out in enumerate((gate_out, up_out)):
        sums = wgrad_send[3, i].astype(F32)
        for slot in range(2):
            sums = sums + wgrad_recv[slot, i].astype(F32)
        out[0] = sums.astype(BF16)
    f_copy.wait_recv()
    row_out[pl.ds(pl.multiple_of(other * half, half), half), :] = fin_recv[...]

    for i in range(3):
        for kind in range(4):
            w_copy(kind, i).wait_send()
    for a in range(2):
        for up in (True, False):
            for k in range(nz - 1):
                pl.when(goes(up, k))(z_copy(up, k, a).wait_send)
            for k in range(1, nz):
                pl.when(comes(up, k))(q_copy(up, k, a, True).wait_send)
    for stage in range(6):
        for i in range(2):
            g_copy(stage, i).wait_send()
    p_copy.wait_send()
    for j in range(1, nz):
        l_copy(j).wait_send()
    f_copy.wait_send()


def dense(
    nz, byte_states, positions, picks, cotangent, router_weight, gate_weight, up_weight, down_weight
):
    rows, width = cotangent.shape
    half, depth, units = rows // 2, gate_weight.shape[1], gate_weight.shape[2]
    spots = positions[None, :]
    vmem, dma = pltpu.VMEM, pltpu.SemaphoreType.DMA
    whole, far = pl.BlockSpec(memory_space=vmem), pl.BlockSpec(memory_space=pl.ANY)
    scratch = [
        vmem((2, nz, half, width + LANES), BF16),
        vmem((2, nz, half, width), BF16),
        vmem((3, 4, depth, units), BF16),
        vmem((3, 2, nz * half, units), F32),
        vmem((2, 2, nz * half, units), BF16),
        vmem((2, nz * half, 1), F32),
        vmem((2, nz * half, LANES), F32),
        vmem((2, nz * half, LANES), BF16),
        vmem((2, nz * half, LANES), BF16),
        vmem((nz, half, width), BF16),
        vmem((nz, half, width), BF16),
        vmem((nz, half, width), F32),
        vmem((nz - 1, half, width), BF16),
        vmem((nz - 1, half, width), BF16),
        vmem((4, 2, depth, units), BF16),
        vmem((3, 2, depth, units), BF16),
        vmem((half, width), BF16),
        vmem((half, width), BF16),
        vmem((LANES, width), BF16),
        vmem(byte_states.shape, BF16),
        vmem((2, nz * half, units), BF16),
        dma((4, 3)), dma((4, 3)),
        dma((2, nz - 1, 2)), dma((2, nz - 1, 2)),
        dma((2, nz - 1, 2)), dma((2, nz - 1, 2)),
        dma, dma,
        dma((nz - 1,)), dma((nz - 1,)),
        dma((6, 2)), dma((6, 2)),
        dma, dma,
        dma((6,)),
    ]
    return pl.pallas_call(
        kernel,
        out_shape=(
            jax.ShapeDtypeStruct((rows, width), BF16),
            jax.ShapeDtypeStruct(gate_weight.shape, BF16),
            jax.ShapeDtypeStruct(up_weight.shape, BF16),
        ),
        in_specs=[far, whole, whole, far, whole, far, far, far],
        out_specs=(whole,) * 3,
        scratch_shapes=scratch,
        compiler_params=pltpu.CompilerParams(
            collective_id=0, has_side_effects=True, vmem_limit_bytes=58 * 2**20
        ),
    )(byte_states, spots, picks.T, cotangent, router_weight.T, gate_weight, up_weight, down_weight)


def local(
    byte_states, positions, picks, cotangent, router_weight, gate_weight, up_weight, down_weight
):
    byte_count = byte_states.shape[0]
    row_total = positions.shape[0]
    width = byte_states.shape[1]
    experts = router_weight.shape[1]
    top_count = picks.shape[1]
    capacity = max(2, 5 * row_total * top_count // (4 * experts))
    pick_total = row_total * top_count
    boundary = jnp.take(byte_states, positions % byte_count, axis=0)
    logits = jnp.dot(boundary, router_weight, preferred_element_type=jnp.float32)
    picked = jnp.take_along_axis(logits, picks, axis=1)
    leading = jax.nn.sigmoid(picked[:, 0] - picked[:, 1])
    mixing = jnp.stack([leading, 1.0 - leading], axis=1)
    mix_low = mixing.astype(jnp.bfloat16).reshape(-1)
    flat_picks = picks.reshape(-1)
    expert_ids = jnp.arange(experts, dtype=jnp.int32)
    one_hot = (flat_picks[:, None] == expert_ids[None, :]).astype(jnp.int32)
    order = jnp.arange(pick_total, dtype=jnp.int32)
    earlier = (order[None, :] < order[:, None]).astype(jnp.bfloat16)
    before = jnp.dot(earlier, one_hot.astype(jnp.bfloat16), preferred_element_type=jnp.float32)
    slot_rank = jnp.sum(before.astype(jnp.int32) * one_hot, axis=1)
    target = flat_picks * capacity + slot_rank
    slot_source = jnp.full((experts * capacity,), pick_total, jnp.int32)
    slot_source = slot_source.at[target].set(jnp.arange(pick_total, dtype=jnp.int32))
    is_live = slot_source < pick_total
    clamped = jnp.minimum(slot_source, pick_total - 1)
    source_row = clamped // top_count
    send_rows = jnp.where(is_live[:, None], boundary[source_row], 0).reshape(
        experts, capacity, width
    )
    send_cot = jnp.where(is_live[:, None], cotangent[source_row], 0).reshape(
        experts, capacity, width
    )
    send_mix = jnp.where(is_live, mix_low[clamped], 0).reshape(experts, capacity)
    gate_full, up_full, down_full = (
        lax.all_gather(gate_weight, "dp", axis=1, tiled=True),
        lax.all_gather(up_weight, "dp", axis=1, tiled=True),
        lax.all_gather(down_weight, "dp", axis=1, tiled=True),
    )
    hidden_half = gate_full.shape[2]
    gate_up = jnp.concatenate([gate_full[0], up_full[0]], axis=1)
    down_mat = down_full[0]
    recv_rows, recv_cot, recv_mix = (
        lax.all_to_all(send_rows, "expert", split_axis=0, concat_axis=0, tiled=True),
        lax.all_to_all(send_cot, "expert", split_axis=0, concat_axis=0, tiled=True),
        lax.all_to_all(send_mix, "expert", split_axis=0, concat_axis=0, tiled=True),
    )
    sources = recv_rows.shape[0]
    slot_total = sources * capacity
    expert_rows = recv_rows.reshape(slot_total, width)
    expert_cot = recv_cot.reshape(slot_total, width)
    expert_mix = recv_mix.reshape(slot_total)
    both_pre = jnp.dot(expert_rows, gate_up, preferred_element_type=jnp.float32)
    gate_pre = both_pre[:, :hidden_half]
    up_pre = both_pre[:, hidden_half:]
    sigma = jax.nn.sigmoid(gate_pre)
    activ = gate_pre * sigma
    slope = sigma * (1.0 + gate_pre * (1.0 - sigma))
    hidden = (activ * up_pre).astype(jnp.bfloat16)
    cot_down = jnp.dot(expert_cot, down_mat, preferred_element_type=jnp.float32)
    mix_part = jnp.sum(hidden.astype(jnp.float32) * cot_down, axis=1)
    scaled = (expert_mix.astype(jnp.float32)[:, None] * expert_cot.astype(jnp.float32)).astype(
        jnp.bfloat16
    )
    hidden_grad = jnp.dot(scaled, down_mat, preferred_element_type=jnp.float32)
    gate_pre_grad = (hidden_grad * up_pre * slope).astype(jnp.bfloat16)
    up_pre_grad = (hidden_grad * activ).astype(jnp.bfloat16)
    joined = jnp.concatenate([gate_pre_grad, up_pre_grad], axis=1)
    grad_part = lax.dot_general(
        joined, gate_up, (((1,), (1,)), ((), ())), preferred_element_type=jnp.float32
    )
    weight_sum = lax.psum_scatter(
        lax.dot_general(
            expert_rows, joined, (((0,), (0,)), ((), ())), preferred_element_type=jnp.float32
        ).astype(jnp.bfloat16),
        "dp",
        scatter_dimension=0,
        tiled=True,
    ).astype(jnp.float32)
    gate_grad = weight_sum[:, :hidden_half].astype(jnp.bfloat16)[None]
    up_grad = weight_sum[:, hidden_half:].astype(jnp.bfloat16)[None]
    grad_sum, mix_sum = (
        lax.psum(grad_part.astype(jnp.bfloat16), "pair").astype(jnp.float32),
        lax.psum(mix_part.astype(jnp.bfloat16), "pair").astype(jnp.float32),
    )
    grad_low = grad_sum.astype(jnp.bfloat16).reshape(sources, capacity, width)
    mix_grad_low = mix_sum.astype(jnp.bfloat16).reshape(sources, capacity)
    back_grad, back_mix = (
        lax.all_to_all(grad_low, "expert", split_axis=0, concat_axis=0, tiled=True),
        lax.all_to_all(mix_grad_low, "expert", split_axis=0, concat_axis=0, tiled=True),
    )
    pick_grad = back_grad.reshape(experts * capacity, width)[target]
    row_sum = jnp.sum(pick_grad.reshape(row_total, top_count, width).astype(jnp.float32), axis=1)
    mix_grad = (
        back_mix.reshape(experts * capacity)[target]
        .reshape(row_total, top_count)
        .astype(jnp.float32)
    )
    blended = jnp.sum(mixing * mix_grad, axis=1, keepdims=True)
    logit_grad = mixing * (mix_grad - blended)
    pick_hot = one_hot.reshape(row_total, top_count, experts).astype(jnp.float32)
    coeffs = jnp.sum(logit_grad[:, :, None] * pick_hot, axis=1)
    router_term = jnp.dot(
        coeffs, router_weight.astype(jnp.float32).T, precision=lax.Precision.HIGHEST
    )
    row_grad = (row_sum + router_term).astype(jnp.bfloat16)
    return (row_grad, gate_grad, up_grad)


def solution(mesh):
    in_specs = (
        P(("expert", "dp"), None),
        P(("expert", "dp")),
        P(("expert", "dp"), None),
        P(("expert", "dp"), None),
        P(),
        P("expert", "dp", "pair"),
        P("expert", "dp", "pair"),
        P("expert", "dp", "pair"),
    )
    out_specs = (P(("expert", "dp"), None), P("expert", "dp", "pair"), P("expert", "dp", "pair"))
    few = dict(mesh.shape) == {"expert": 4, "dp": 4, "pair": 2}
    body = functools.partial(dense, 4) if few else local
    return jax.shard_map(body, mesh=mesh, in_specs=in_specs, out_specs=out_specs, check_vma=False)
```
